32 devices in a mesh: rep: 2 (over y), shard: 4 (over z), seq: 4 (over x, core).
Axes of the slice: x: 2, y: 2, z: 4, core: 2. Of those that a mesh axis runs over, the one named last changes fastest.
Arguments:
- tokens: bfloat16 [32768, 768], P(('rep', 'shard', 'seq')), may hold values from -6 to 6
- doc_lengths: int32 [8, 4], P(('rep', 'shard')), may hold values from 1 to 3584, as said below
- expert_ids: int32 [32768, 1], P(('rep', 'shard', 'seq')), may hold values from 0 to 15; in each aligned block of 1024 rows (0 to 1023, 1024 to 2047, ...) at most 80 rows name the same one
- cotangent: bfloat16 [32768, 768], P(('rep', 'shard', 'seq')), may hold values from -6 to 6
- gain_attn: bfloat16 [768], P(('shard', 'seq')), may hold values from 0.5 to 1.5
- gain_ffn: bfloat16 [768], P(('shard', 'seq')), may hold values from 0.5 to 1.5
- w_query: bfloat16 [768, 768], P(('shard', 'seq')), may hold values from -0.078125 to 0.078125
- w_key: bfloat16 [768, 768], P(('shard', 'seq')), may hold values from -0.078125 to 0.078125
- w_value: bfloat16 [768, 768], P(('shard', 'seq')), may hold values from -0.21875 to 0.21875
- w_attn_out: bfloat16 [768, 768], P(('shard', 'seq')), may hold values from -3.5 to 3.5
- rel_table: bfloat16 [32, 12], P(('shard', 'seq')), may hold values from -4 to 4
- w_router: bfloat16 [768, 16], P(('shard', 'seq')), may hold values from -0.15625 to 0.15625
- w_expert_in: bfloat16 [16, 768, 3072], P(('shard', 'seq')), may hold values from -0.21875 to 0.21875
- w_expert_out: bfloat16 [16, 3072, 768], P(('shard', 'seq')), may hold values from -1.75 to 1.75
Outputs:
- mixed: bfloat16 [32768, 768], P(('rep', 'shard', 'seq'))
- loss: float32 [], replicated
- importance: float32 [16], replicated
- d_tokens: float32 [32768, 768], P(('rep', 'shard', 'seq'))
- d_gain_attn: float32 [768], P(('shard', 'seq'))
- d_gain_ffn: float32 [768], P(('shard', 'seq'))
- d_query: float32 [768, 768], P(('shard', 'seq'))
- d_key: float32 [768, 768], P(('shard', 'seq'))
- d_value: float32 [768, 768], P(('shard', 'seq'))
- d_attn_out: float32 [768, 768], P(('shard', 'seq'))
- d_rel_table: float32 [32, 12], P(('shard', 'seq'))
- d_router: float32 [768, 16], P(('shard', 'seq'))
- d_expert_in: float32 [16, 768, 3072], P(('shard', 'seq'))
- d_expert_out: float32 [16, 3072, 768], P(('shard', 'seq'))
The draws below stay inside these ranges and needn't reach their ends.
Inputs may be any that keep to these rules, and one draw needn't show every extreme that they name: `doc_lengths`: in each sequence one document has exactly 3584 positions; the lengths sum to less than 4096; sequence 0 has a document of 1 position. `expert_ids`: among the rows of one device at most 80 name the same expert.
All inputs are finite; a program needn't handle non-finite values.
Results may differ from the reference program's by a relative error of at most 0.02.
Values may be sent and summed in bfloat16 or wider, within the bound.
No kernel may reach another device: no remote copies, remote signals or barrier semaphores. Data moves between devices by JAX's collectives and lax.ppermute only.
A program may use at most 384 MiB of HBM per device.

```python
import math
import jax
import jax.numpy as jnp
import numpy as np
from jax import lax

D = 768
HEADS = 12
HEAD = 64
FF = 3072
BUCKETS = 32
MAXDIST = 128
WINDOW = 1024
DOCS = 4
TOK_DEV = 1024
EXPERTS = 16
SEQ = 4096
SEQS = 8
TOKENS = 32768
CAP = 80
N_SEQ = 4


def draw_doc_lengths(key, part):
    key = jax.random.fold_in(key, 11)
    key_short = jax.random.fold_in(key, 1)
    key_place = jax.random.fold_in(key, 2)
    remainder = TOK_DEV // 2
    longest = SEQ - remainder
    short_docs = jax.random.randint(key_short, (SEQS, DOCS - 1), 1, remainder // DOCS + 1)
    corner = (jnp.arange(SEQS, dtype=jnp.int32)[:, None] == 0) & (jnp.arange(DOCS - 1, dtype=jnp.int32)[None, :] == 0)
    short_docs = jnp.where(corner, 1, short_docs)
    big_index = jax.random.randint(key_place, (SEQS, 1), 0, DOCS)
    column = jnp.arange(DOCS, dtype=jnp.int32)[None, :]
    shifted_left = jnp.concatenate([short_docs, short_docs[:, -1:]], axis=1)
    shifted_right = jnp.concatenate([short_docs[:, :1], short_docs], axis=1)
    lengths = jnp.where(column < big_index, shifted_left, jnp.where(column == big_index, longest, shifted_right))
    return lengths.astype(jnp.int32)


def steps_of(own_key, dims, shards, least, high):
    loudness = 1.0
    for axis_at, shards_of in shards:
        heights = jax.random.uniform(jax.random.fold_in(jax.random.fold_in(own_key, 6), axis_at), (shards_of,), jnp.float32, least / len(shards), high / len(shards))
        loudness = loudness * jnp.repeat(jnp.exp(heights), dims[axis_at] // shards_of).reshape((-1,) + (1,) * (len(dims) - 1 - axis_at))
    return loudness


def deal_out(key, own, number, rows, count, top, bound, slope):
    ranking = jax.random.permutation(key, count)
    crowded, ordinary = load_shares(count, rows * top, bound, slope, True), load_shares(count, rows * top, bound, slope, False)
    places = jnp.arange(count)

    def named(sizes, offset_by):
        used = int((sizes > 0).sum())
        fixed = max(1, used // 4)
        shifted = fixed + (places - fixed + offset_by * (used - fixed)) % max(1, count - fixed)
        return jnp.zeros((count,), jnp.int32).at[ranking[jnp.where(places < fixed, places, shifted)]].set(jnp.asarray(sizes, jnp.int32))

    sizes = jnp.where(number % 4 == 0, named(crowded, number // 4), named(ordinary, number - number // 4 - 1))
    mixed = jax.random.permutation(jax.random.fold_in(own, 3), count)
    donor, taker = mixed[0:count // 2 * 2:2], mixed[1:count // 2 * 2:2]
    room = jnp.minimum(sizes[donor] - 1, bound - sizes[taker]) // 2
    room = jnp.where((donor == ranking[0]) | (taker == ranking[0]) | (sizes[taker] == 0), 0, jnp.maximum(room, 0))
    shifted = jax.random.randint(jax.random.fold_in(own, 4), (count // 2,), 0, 1 << 20) % (room + 1)
    sizes = sizes.at[donor].add(-shifted).at[taker].add(shifted)
    items = jnp.searchsorted(jnp.cumsum(sizes), jnp.arange(rows * top), side="right").astype(jnp.int32)
    listing = items.reshape(top, rows).T
    listing = listing[jax.random.permutation(jax.random.fold_in(own, 1), rows)]
    offset_by = jax.random.randint(jax.random.fold_in(own, 2), (rows, 1), 0, top)
    return jnp.take_along_axis(listing, (jnp.arange(top)[None, :] + offset_by) % top, axis=1)


def load_shares(count, total, limit, skew, full):
    portions = [(1 << 20) // math.isqrt(rank ** skew) + 1 for rank in range(1, count + 1)]
    largest = limit if full else min(limit, max(-(-total // count), total * portions[0] // sum(portions)))
    least = 1 if total - largest >= count - 1 else 0
    given, spare = [largest] + [least] * (count - 1), total - largest - least * (count - 1)
    while spare > 0:
        free = [i for i in range(1, count) if given[i] < largest] or [i for i in range(1, count) if given[i] < limit]
        mass, budget = sum([portions[i] for i in free]), spare
        for i in free:
            extra = min(limit - given[i], max(1, budget * portions[i] // mass), spare)
            given[i] = given[i] + extra
            spare = spare - extra
    return np.array(given)


def normal_values(key, dims, width, bound, pieces=(), kind=jnp.bfloat16):
    result = jax.random.normal(key, dims, jnp.float32) * width
    if len(pieces) > 0:
        result = steps_of(key, dims, pieces, -0.22, 0.18) * result
    return jnp.clip(result, min=-bound, max=bound).astype(kind)


def setup_inputs(seed: int = 0) -> dict:
    seeds = jax.random.split(jax.random.key(seed), 15)
    tokens = normal_values(seeds[0], (TOKENS, D), 1.0, 6.0, ((0, 32),))
    doc_lengths = draw_doc_lengths(jax.random.fold_in(seeds[14], 71), 0)
    expert_ids_keys = jax.random.split(jax.random.fold_in(seeds[2], 1), TOKENS // TOK_DEV)
    expert_ids_turns = jax.random.permutation(jax.random.fold_in(seeds[2], 3), TOKENS // TOK_DEV)
    expert_ids = jax.vmap(lambda own, number: deal_out(jax.random.fold_in(seeds[2], 2), own, number, TOK_DEV, EXPERTS, 1, CAP, 1))(expert_ids_keys, expert_ids_turns).reshape((TOKENS, 1))
    cotangent = normal_values(seeds[3], (TOKENS, D), 1.0, 6.0, ((0, 32),))
    gain_attn = jnp.clip(1.0 + 0.1 * jax.random.normal(seeds[4], (D,), jnp.float32), 0.5, 1.5).astype(jnp.bfloat16)
    gain_ffn = jnp.clip(1.0 + 0.1 * jax.random.normal(seeds[5], (D,), jnp.float32), 0.5, 1.5).astype(jnp.bfloat16)
    w_query = normal_values(seeds[6], (D, D), (8 * D) ** -0.5, 0.078125, ((0, 16),))
    w_key = normal_values(seeds[7], (D, D), (8 * D) ** -0.5, 0.078125, ((0, 16),))
    w_value = normal_values(seeds[8], (D, D), D ** -0.5, 0.21875, ((0, 16),))
    w_attn_out = normal_values(seeds[9], (D, D), (D * 4 // WINDOW) ** -0.5, 3.5, ((0, 16),))
    rel_table = normal_values(seeds[10], (BUCKETS, HEADS), 1.0, 4.0, ((0, 16),))
    w_router = normal_values(seeds[11], (D, EXPERTS), (2 * D) ** -0.5, 0.15625, ((0, 16),))
    w_expert_in = normal_values(seeds[12], (EXPERTS, D, FF), D ** -0.5, 0.21875, ((0, 16),))
    w_expert_out = normal_values(seeds[13], (EXPERTS, FF, D), (FF // (EXPERTS * EXPERTS) + 1) ** -0.5, 1.75, ((0, 16),))
    return dict(tokens=tokens, doc_lengths=doc_lengths, expert_ids=expert_ids, cotangent=cotangent, gain_attn=gain_attn, gain_ffn=gain_ffn, w_query=w_query, w_key=w_key, w_value=w_value, w_attn_out=w_attn_out, rel_table=rel_table, w_router=w_router, w_expert_in=w_expert_in, w_expert_out=w_expert_out)


EPSILON = 1e-06
AUX_WEIGHT = 0.01
MASKED_SCORE = -1e+30
PRECISE = lax.Precision.HIGHEST

@jax.custom_vjp
def low(v):
    return lax.optimization_barrier(v.astype(jnp.bfloat16)).astype(jnp.float32)

@jax.custom_vjp
def low_back(v):
    return v

def low_keep(v):
    return (low(v), None)

def low_pass(kept, grad):
    return (grad,)

def back_keep(v):
    return (v, None)

def back_low(kept, grad):
    return (low(grad),)
low.defvjp(low_keep, low_pass)
low_back.defvjp(back_keep, back_low)

def matmul_high(matrix_a, matrix_b):
    return jnp.dot(matrix_a, matrix_b, precision=PRECISE, preferred_element_type=jnp.float32)

def rms_norm(vectors, gains):
    return vectors * lax.rsqrt(lax.optimization_barrier(jnp.mean(vectors * vectors, axis=-1, keepdims=True)) + EPSILON) * gains

def thresholds(max_distance, half_count):
    exact_span = half_count // 2
    collected = list(range(1, exact_span + 1))
    for target_level in range(exact_span + 1, half_count):
        candidate = exact_span
        while exact_span + int(math.log(candidate / exact_span) / math.log(max_distance / exact_span) * (half_count - exact_span)) < target_level:
            candidate += 1
        collected.append(candidate)
    return collected

def bucket_of(distance, half_count, limits):
    magnitude = jnp.abs(distance)
    bucket_id = (distance > 0).astype(jnp.int32) * half_count
    for boundary in limits:
        bucket_id = bucket_id + (magnitude >= boundary).astype(jnp.int32)
    return bucket_id

def attend(seq_tokens, seq_lengths, gain_attn, w_query, w_key, w_value, w_attn_out, rel_table):
    normed_one = low(rms_norm(seq_tokens, gain_attn))
    queries = low(low_back(matmul_high(normed_one, w_query))).reshape(SEQ, HEADS, HEAD)
    key_rows = low(low_back(matmul_high(normed_one, w_key))).reshape(SEQ, HEADS, HEAD)
    values = low(low_back(matmul_high(normed_one, w_value))).reshape(SEQ, HEADS, HEAD)
    doc_ends = jnp.cumsum(seq_lengths).astype(jnp.int32)
    places = jnp.arange(SEQ, dtype=jnp.int32)
    doc_ids = lax.optimization_barrier(jnp.sum((places[:, None] >= doc_ends[None, :]).astype(jnp.int32), axis=1)).astype(jnp.int32)
    is_live = places < doc_ends[DOCS - 1]
    limits = thresholds(MAXDIST, BUCKETS // 2)
    block_rows = min(512, TOK_DEV)
    half_window = WINDOW // 2

    def rows_of(first_row):
        q_places = first_row + jnp.arange(block_rows, dtype=jnp.int32)
        q_block = lax.dynamic_slice_in_dim(queries, first_row, block_rows, 0)
        distance = places[None, :] - q_places[:, None]
        buckets = bucket_of(distance, BUCKETS // 2, limits)
        rel_bias = jnp.transpose(rel_table[buckets], (2, 0, 1))
        scores = low_back(jnp.einsum('qhd,khd->hqk', q_block, key_rows, precision=PRECISE) + rel_bias)
        q_docs = lax.dynamic_slice_in_dim(doc_ids, first_row, block_rows, 0)
        allowed = (q_docs[:, None] == doc_ids[None, :]) & is_live[None, :] & (jnp.abs(distance) <= half_window) | (distance == 0)
        scores = jnp.where(allowed[None], scores, MASKED_SCORE)
        weights = low(jax.nn.softmax(scores, axis=-1))
        return jnp.einsum('hqk,khd->qhd', weights, values, precision=PRECISE)
    starts = jnp.arange(SEQ // block_rows, dtype=jnp.int32) * block_rows
    context = lax.map(jax.checkpoint(rows_of), starts).reshape(SEQ, D)
    context = low(low_back(context))
    return seq_tokens + low_back(matmul_high(context, w_attn_out))

def reference(tokens, doc_lengths, expert_ids, cotangent, gain_attn, gain_ffn, w_query, w_key, w_value, w_attn_out, rel_table, w_router, w_expert_in, w_expert_out):
    doc_ends = jnp.cumsum(doc_lengths, axis=1).astype(jnp.int32)
    places = jnp.arange(SEQ, dtype=jnp.int32)
    is_live = (places[None, :] < doc_ends[:, DOCS - 1:DOCS]).reshape(TOKENS)
    live_int = is_live.astype(jnp.int32)
    chosen_ids = expert_ids[:, 0].astype(jnp.int32)
    chosen = (chosen_ids[:, None] == jnp.arange(EXPERTS, dtype=jnp.int32)[None, :]).astype(jnp.int32) * live_int[:, None]
    chosen_f = chosen.astype(jnp.float32)
    live_f = is_live.astype(jnp.float32)
    counts = lax.optimization_barrier(jnp.sum(chosen_f, axis=0))
    live_count = jnp.sum(counts)
    shares = counts / live_count
    ranked = jnp.cumsum(chosen, axis=0).astype(jnp.int32)
    slot_index = (lax.optimization_barrier(jnp.sum(ranked * chosen, axis=1)) - 1).astype(jnp.int32)
    slot_depth = CAP * SEQS * N_SEQ
    target = jnp.where(is_live, chosen_ids * slot_depth + slot_index, EXPERTS * slot_depth).astype(jnp.int32)

    def layer_forward(inputs, g_attn, g_ffn, wq, wk, wv, wo, table, router, w_in, w_out):
        sequences = inputs.reshape(SEQS, SEQ, D)

        def per_sequence(member):
            return attend(member[0], member[1], g_attn, wq, wk, wv, wo, table)
        hidden_state = lax.map(jax.checkpoint(per_sequence), (sequences, doc_lengths)).reshape(TOKENS, D)
        normed = low(rms_norm(hidden_state, g_ffn))
        router_logits = low_back(matmul_high(normed, router))
        router_probs = jax.nn.softmax(router_logits, axis=-1)
        gating = lax.optimization_barrier(jnp.sum(router_probs * chosen_f, axis=1))
        routed = low_back(normed)
        buffer_rows = jnp.zeros((EXPERTS * slot_depth + 1, D), jnp.float32).at[target].add(routed)
        buffer_rows = buffer_rows[:EXPERTS * slot_depth].reshape(EXPERTS, slot_depth, D)

        def expert(member):
            pre_act = low_back(matmul_high(member[0], member[1]))
            inner_act = low(jax.nn.gelu(pre_act, approximate=True))
            return low(low_back(matmul_high(inner_act, member[2])))
        expert_out = lax.map(jax.checkpoint(expert), (buffer_rows, w_in, w_out))
        flattened = jnp.concatenate([expert_out.reshape(EXPERTS * slot_depth, D), jnp.zeros((1, D), jnp.float32)], axis=0)
        mixed = hidden_state + gating[:, None] * flattened[target]
        balance = EXPERTS * jnp.sum(live_f * matmul_high(router_probs, shares)) / live_count
        importance = EXPERTS * lax.optimization_barrier(jnp.sum(live_f[:, None] * router_probs, axis=0)) / TOKENS
        return (mixed, balance, importance)
    floats = (tokens.astype(jnp.float32), gain_attn.astype(jnp.float32), gain_ffn.astype(jnp.float32), w_query.astype(jnp.float32), w_key.astype(jnp.float32), w_value.astype(jnp.float32), w_attn_out.astype(jnp.float32), rel_table.astype(jnp.float32), w_router.astype(jnp.float32), w_expert_in.astype(jnp.float32), w_expert_out.astype(jnp.float32))
    outputs, pullback = jax.vjp(layer_forward, *floats)
    grads = pullback((cotangent.astype(jnp.float32), jnp.asarray(AUX_WEIGHT, jnp.float32), jnp.zeros((EXPERTS,), jnp.float32)))
    return (outputs[0].astype(jnp.bfloat16), outputs[1], outputs[2], grads[0], grads[1], grads[2], grads[3], grads[4], grads[5], grads[6], grads[7], grads[8], grads[9], grads[10])
```

```python
import functools
import math

import jax
import jax.numpy as jnp
import numpy as np
from jax import lax
from jax.experimental import pallas as pl
from jax.experimental.pallas import tpu as pltpu
from jax.sharding import PartitionSpec as P

D = 768
HEADS = 12
HEAD = 64
BUCKETS = 32
MAXDIST = 128
WINDOW = 1024
DOCS = 4
MASKED_SCORE = -1e30
HALF = WINDOW // 2
QB = 256
SUB = 128
KB = QB + WINDOW
PAIRS = HEADS // 2
VMEM_LIMIT = 56 * 1024 * 1024


def thresholds(max_distance, half_count):
    exact_span = half_count // 2
    collected = list(range(1, exact_span + 1))
    for target_level in range(exact_span + 1, half_count):
        candidate = exact_span
        while (
            exact_span
            + int(
                math.log(candidate / exact_span)
                / math.log(max_distance / exact_span)
                * (half_count - exact_span)
            )
            < target_level
        ):
            candidate += 1
        collected.append(candidate)
    return collected


LIMITS = thresholds(MAXDIST, BUCKETS // 2)
assert LIMITS[-1] <= SUB


def bucket_table(distance):
    distance = np.asarray(distance)
    magnitude = np.abs(distance)
    bucket_id = (distance > 0).astype(np.int32) * (BUCKETS // 2)
    for boundary in LIMITS:
        bucket_id = bucket_id + (magnitude >= boundary)
    return bucket_id


def bias_buckets():
    lane = np.arange(2 * SUB)
    rows = []
    for m in (-1, 0, 1):
        rows.append(bucket_table(SUB * m - lane + np.where(lane >= SUB, 2 * SUB, 0)))
    rows.append(np.full(2 * SUB, bucket_table(-WINDOW)))
    rows.append(np.full(2 * SUB, bucket_table(WINDOW)))
    rows += [np.zeros(2 * SUB, np.int32)] * 3
    return np.stack(rows)


def grad_buckets():
    lane = np.arange(SUB)
    rows = [bucket_table(SUB * m - lane) for m in (-1, 0, 1)]
    rows += [bucket_table(SUB * (m + 1) - lane) for m in (-1, 0, 1)]
    rows.append(np.full(SUB, bucket_table(-WINDOW)))
    rows.append(np.full(SUB, bucket_table(WINDOW)))
    return np.stack(rows)


def one_hot(ids):
    return (ids[..., None] == np.arange(BUCKETS)).astype(np.float32)


def dot(a, b):
    return jnp.dot(a, b, preferred_element_type=jnp.float32)


def dot_nt(a, b):
    return lax.dot_general(a, b, (((1,), (1,)), ((), ())), preferred_element_type=jnp.float32)


def head_lanes(shape, axis, h):
    place = lax.broadcasted_iota(jnp.int32, shape, axis)
    return (place < HEAD) if h == 0 else (place >= HEAD)


def fold8(x, op):
    return op(x.reshape(x.shape[0] // 8, 8, x.shape[1]), axis=0)


def forward_kernel(
    q_ref, k_ref, v_ref, qf_ref, kf_ref, live_ref, w_ref, ctx_ref, e_ref, inv_ref, vt, bias, s_ref
):
    step = pl.program_id(1)

    @pl.when(step == 0)
    def _():
        for s in range(v_ref.shape[0] // QB):
            vt[:, s * QB : (s + 1) * QB] = v_ref[s * QB : (s + 1) * QB, :].T
        for h in range(2):
            for m in range(3):
                row = jnp.broadcast_to(w_ref[h, m : m + 1, :], (SUB, 2 * SUB))
                bias[h, m] = pltpu.roll(row, 0, 1, stride=1, stride_axis=0)[:, :SUB]

    base = pl.multiple_of(step * QB, QB)
    q = q_ref[...]
    qf = qf_ref[...]
    row_id = lax.broadcasted_iota(jnp.int32, (SUB, SUB), 0)
    col_id = lax.broadcasted_iota(jnp.int32, (SUB, SUB), 1)
    contexts = []
    for h in range(2):
        qx = jnp.concatenate([jnp.where(head_lanes(q.shape, 1, h), q, 0), qf], axis=1)
        neg = w_ref[h, 3:4, :SUB]
        pos = w_ref[h, 4:5, :SUB]
        tops = {(b, kind): None for b in range(2) for kind in "nvp"}
        for c in range(KB // QB):
            place = pl.multiple_of(base + c * QB, QB)
            kx = jnp.concatenate([k_ref[pl.ds(place, QB), :], kf_ref[pl.ds(place, QB), :]], axis=1)
            st = dot_nt(kx, qx)
            for a in range(2 * c, 2 * c + 2):
                for b in range(2):
                    m = a - b - 4
                    if abs(m) > 4:
                        continue
                    x = st[(a - 2 * c) * SUB : (a - 2 * c + 1) * SUB, b * SUB : (b + 1) * SUB]
                    if m == -4:
                        x = jnp.where(row_id >= col_id, x, MASKED_SCORE)
                    if m == 4:
                        x = jnp.where(row_id <= col_id, x, MASKED_SCORE)
                    if abs(m) <= 1:
                        x = x + bias[h, m + 1]
                    s_ref[h, a * SUB : (a + 1) * SUB, b * SUB : (b + 1) * SUB] = x
                    kind = "n" if m < -1 else "p" if m > 1 else "v"
                    top = fold8(x, jnp.max)
                    old = tops[b, kind]
                    tops[b, kind] = top if old is None else jnp.maximum(old, top)
        peaks = []
        for b in range(2):
            peak = jnp.maximum(
                jnp.maximum(tops[b, "n"] + neg, tops[b, "p"] + pos), tops[b, "v"]
            )
            peaks.append(jnp.max(peak, axis=0, keepdims=True))
        totals = [jnp.zeros((8, SUB), jnp.float32)] * 2
        ct = jnp.zeros((HEAD, QB), jnp.float32)
        for c in range(KB // QB):
            for a in range(2 * c, 2 * c + 2):
                for b in range(2):
                    m = a - b - 4
                    rows = slice(a * SUB, (a + 1) * SUB)
                    cols = slice(b * SUB, (b + 1) * SUB)
                    if abs(m) > 4:
                        e_ref[0, 0, h, rows, cols] = jnp.zeros((SUB, SUB), jnp.bfloat16)
                        continue
                    peak = peaks[b]
                    if m < -1:
                        peak = peak - neg
                    if m > 1:
                        peak = peak - pos
                    e = jnp.exp(s_ref[h, rows, cols] - peak)
                    totals[b] = totals[b] + fold8(e, jnp.sum)
                    e_ref[0, 0, h, rows, cols] = e.astype(jnp.bfloat16)
            place = pl.multiple_of(base + c * QB, QB)
            ct = ct + dot(
                vt[h * HEAD : (h + 1) * HEAD, pl.ds(place, QB)],
                e_ref[0, 0, h, c * QB : (c + 1) * QB, :],
            )
        total = jnp.concatenate([jnp.sum(t, axis=0, keepdims=True) for t in totals], axis=1)
        inv = 1.0 / total
        inv_ref[0, 0, h : h + 1, :] = inv
        contexts.append(ct * inv)
    context = jnp.concatenate(contexts, axis=0).T.astype(jnp.bfloat16)
    own = v_ref[pl.ds(pl.multiple_of(base + HALF, QB), QB), :]
    ctx_ref[...] = jnp.where(live_ref[...] > 0, context, own)


def backward_kernel(
    q_ref,
    k_ref,
    v_ref,
    live_ref,
    e_ref,
    inv_ref,
    ctx_ref,
    dctx_ref,
    dq_ref,
    dk_ref,
    dv_ref,
    db_ref,
    kt,
    dk_acc,
    dv_acc,
    acc,
    far,
):
    step = pl.program_id(1)

    @pl.when(step == 0)
    def _():
        for s in range(k_ref.shape[0] // QB):
            kt[:, s * QB : (s + 1) * QB] = k_ref[s * QB : (s + 1) * QB, :].T
        dk_acc[...] = jnp.zeros_like(dk_acc)
        dv_acc[...] = jnp.zeros_like(dv_acc)
        acc[...] = jnp.zeros_like(acc)
        far[...] = jnp.zeros_like(far)

    base = pl.multiple_of(step * QB, QB)
    q = q_ref[...]
    dctx = dctx_ref[...].astype(jnp.float32)
    is_live = live_ref[...] > 0
    kept = jnp.where(is_live, dctx, 0.0)
    prod = (kept * ctx_ref[...].astype(jnp.float32)).T
    kept_t = kept.T
    qs, dts, deltas = [], [], []
    for h in range(2):
        inv = inv_ref[0, 0, h : h + 1, :]
        qs.append(jnp.where(head_lanes(q.shape, 1, h), q, 0))
        dts.append(
            jnp.where(head_lanes(kept_t.shape, 0, h), kept_t * inv, 0.0).astype(jnp.bfloat16)
        )
        deltas.append(
            jnp.sum(prod[h * HEAD : (h + 1) * HEAD], axis=0, keepdims=True) * inv
        )
    q_both = jnp.concatenate(qs, axis=0)
    dt_both = jnp.concatenate(dts, axis=1)
    fars = [[jnp.zeros((8, SUB), jnp.float32)] * 2 for _ in range(2)]
    dqt = [jnp.zeros((HEAD, QB), jnp.float32)] * 2
    for c in range(KB // QB):
        place = pl.multiple_of(base + c * QB, QB)
        vc = v_ref[pl.ds(place, QB), :]
        grads, weights = [], []
        for h in range(2):
            dp = dot(vc, dts[h])
            e = e_ref[0, 0, h, c * QB : (c + 1) * QB, :]
            ds = e.astype(jnp.float32) * (dp - deltas[h])
            for a in range(2 * c, 2 * c + 2):
                for b in range(2):
                    m = a - b - 4
                    x = ds[(a - 2 * c) * SUB : (a - 2 * c + 1) * SUB, b * SUB : (b + 1) * SUB]
                    if abs(m) > 4:
                        continue
                    if abs(m) <= 1:
                        acc[h, m + 1] += x
                    else:
                        side = 0 if m < 0 else 1
                        fars[h][side] = fars[h][side] + fold8(x, jnp.sum)
            ds = ds.astype(jnp.bfloat16)
            dqt[h] = dqt[h] + dot(kt[h * HEAD : (h + 1) * HEAD, pl.ds(place, QB)], ds)
            grads.append(ds)
            weights.append(e)
        dk_acc[pl.ds(place, QB), :] += dot(jnp.concatenate(grads, axis=1), q_both)
        dv_acc[pl.ds(place, QB), :] += dot_nt(jnp.concatenate(weights, axis=1), dt_both)
    dq_ref[...] = jnp.concatenate(dqt, axis=0).T.astype(jnp.bfloat16)
    own = pl.ds(pl.multiple_of(base + HALF, QB), QB)
    dv_acc[own, :] += dctx - kept
    for h in range(2):
        for side in range(2):
            far[h, side] += fars[h][side]

    @pl.when(step == pl.num_programs(1) - 1)
    def _():
        dk_ref[...] = dk_acc[...].astype(jnp.bfloat16)
        dv_ref[...] = dv_acc[...].astype(jnp.bfloat16)
        row_id = lax.broadcasted_iota(jnp.int32, (SUB, SUB), 0)
        col_id = lax.broadcasted_iota(jnp.int32, (SUB, SUB), 1)
        sublane = lax.broadcasted_iota(jnp.int32, (8, SUB), 0)
        for h in range(2):
            sums = []
            for upper in (True, False):
                for m in range(3):
                    x = jnp.where((col_id >= row_id) == upper, acc[h, m], 0.0)
                    y = x[:8]
                    for g in range(1, SUB // 8):
                        y = y + pltpu.roll(x[8 * g : 8 * g + 8], SUB - 8 * g, 1)
                    for bit in range(3):
                        y = jnp.where(
                            (sublane >> bit) % 2 == 1, pltpu.roll(y, SUB - (1 << bit), 1), y
                        )
                    sums.append(jnp.sum(y, axis=0, keepdims=True))
            for side in range(2):
                sums.append(jnp.sum(far[h, side], axis=0, keepdims=True))
            db_ref[h] = jnp.concatenate(sums, axis=0)


def spec(shape, index):
    return pl.BlockSpec(shape, index)


def attention_forward(queries, key_value, q_feat, k_feat, live, bias_rows):
    rows, span = queries.shape[0], key_value.shape[0]
    steps = rows // QB
    return pl.pallas_call(
        forward_kernel,
        grid=(PAIRS, steps),
        in_specs=[
            spec((QB, SUB), lambda p, i: (i, p)),
            spec((span, SUB), lambda p, i: (0, p)),
            spec((span, SUB), lambda p, i: (0, p + PAIRS)),
            spec((QB, SUB), lambda p, i: (i, 0)),
            spec((span, SUB), lambda p, i: (0, 0)),
            spec((QB, SUB), lambda p, i: (i, 0)),
            spec((2, 8, 2 * SUB), lambda p, i: (p, 0, 0)),
        ],
        out_specs=[
            spec((QB, SUB), lambda p, i: (i, p)),
            spec((1, 1, 2, KB, QB), lambda p, i: (p, i, 0, 0, 0)),
            spec((1, 1, 8, QB), lambda p, i: (p, i, 0, 0)),
        ],
        out_shape=[
            jax.ShapeDtypeStruct((rows, D), jnp.bfloat16),
            jax.ShapeDtypeStruct((PAIRS, steps, 2, KB, QB), jnp.bfloat16),
            jax.ShapeDtypeStruct((PAIRS, steps, 8, QB), jnp.float32),
        ],
        scratch_shapes=[
            pltpu.VMEM((SUB, span), jnp.bfloat16),
            pltpu.VMEM((2, 3, SUB, SUB), jnp.float32),
            pltpu.VMEM((2, KB, QB), jnp.float32),
        ],
        compiler_params=pltpu.CompilerParams(
            dimension_semantics=("arbitrary", "arbitrary"), vmem_limit_bytes=VMEM_LIMIT
        ),
        cost_estimate=pl.CostEstimate(
            flops=4 * rows * KB * D * 4, bytes_accessed=45_000_000, transcendentals=rows * KB * HEADS
        ),
    )(queries, key_value, key_value, q_feat, k_feat, live, bias_rows)


def attention_backward(
    queries, key_value, live, expo, inverse, context, d_context, first, pairs
):
    rows, span = queries.shape[0], key_value.shape[0]
    steps = rows // QB
    return pl.pallas_call(
        backward_kernel,
        grid=(pairs, steps),
        in_specs=[
            spec((QB, SUB), lambda p, i: (i, p + first)),
            spec((span, SUB), lambda p, i: (0, p + first)),
            spec((span, SUB), lambda p, i: (0, p + first + PAIRS)),
            spec((QB, SUB), lambda p, i: (i, 0)),
            spec((1, 1, 2, KB, QB), lambda p, i: (p + first, i, 0, 0, 0)),
            spec((1, 1, 8, QB), lambda p, i: (p + first, i, 0, 0)),
            spec((QB, SUB), lambda p, i: (i, p + first)),
            spec((QB, SUB), lambda p, i: (i, p + first)),
        ],
        out_specs=[
            spec((QB, SUB), lambda p, i: (i, p)),
            spec((span, SUB), lambda p, i: (0, p)),
            spec((span, SUB), lambda p, i: (0, p)),
            spec((2, 8, SUB), lambda p, i: (p, 0, 0)),
        ],
        out_shape=[
            jax.ShapeDtypeStruct((rows, pairs * SUB), jnp.bfloat16),
            jax.ShapeDtypeStruct((span, pairs * SUB), jnp.bfloat16),
            jax.ShapeDtypeStruct((span, pairs * SUB), jnp.bfloat16),
            jax.ShapeDtypeStruct((2 * pairs, 8, SUB), jnp.float32),
        ],
        scratch_shapes=[
            pltpu.VMEM((SUB, span), jnp.bfloat16),
            pltpu.VMEM((span, SUB), jnp.float32),
            pltpu.VMEM((span, SUB), jnp.float32),
            pltpu.VMEM((2, 3, SUB, SUB), jnp.float32),
            pltpu.VMEM((2, 2, 8, SUB), jnp.float32),
        ],
        compiler_params=pltpu.CompilerParams(
            dimension_semantics=("arbitrary", "arbitrary"), vmem_limit_bytes=VMEM_LIMIT
        ),
        cost_estimate=pl.CostEstimate(
            flops=8 * rows * KB * pairs * SUB * 4, bytes_accessed=9_000_000 * pairs, transcendentals=0
        ),
    )(queries, key_value, key_value, live, expo, inverse, context, d_context)


FF = 3072
TILE = 256


def gelu_parts(v):
    scale = 0.7978845608
    square = v * v
    t = jnp.tanh(scale * v * (1.0 + 0.044715 * square))
    half = 0.5 * (1.0 + t)
    slope = half + 0.5 * v * (1.0 - t * t) * (scale + (3 * 0.044715 * scale) * square)
    return half * v, slope


def routing(x, router, pick, experts):
    logits = dot(x, router)
    lane = lax.broadcasted_iota(jnp.int32, logits.shape, 1)
    logits = jnp.where(lane < experts, logits, MASKED_SCORE)
    expo = jnp.exp(logits - jnp.max(logits, axis=1, keepdims=True))
    probs = expo / jnp.sum(expo, axis=1, keepdims=True)
    return probs, jnp.sum(probs * pick, axis=1, keepdims=True)


def hidden_pair(x, d_rows, w_in, w_out):
    inner, slope = gelu_parts(dot(x, w_in))
    d_pre = dot_nt(d_rows, w_out) * slope
    return inner.astype(jnp.bfloat16), d_pre.astype(jnp.bfloat16)


def row_chunks(rows):
    return [slice(s, s + QB) for s in range(0, rows, QB)]


def expert_kernel(
    experts,
    x_ref,
    c_ref,
    router_ref,
    pick_ref,
    aux_ref,
    win_ref,
    wout_ref,
    rows_ref,
    back_ref,
    act_ref,
    dpre_ref,
    drows_ref,
    dlog_ref,
    probs,
    rows_acc,
    back_acc,
):
    step = pl.program_id(0)
    pick = pick_ref[0:1, :]

    @pl.when(step == 0)
    def _():
        for r in row_chunks(x_ref.shape[0]):
            p, gate = routing(x_ref[r, :], router_ref[...], pick, experts)
            probs[r, :] = p
            drows_ref[r, :] = (gate * c_ref[r, :].astype(jnp.float32)).astype(jnp.bfloat16)
        rows_acc[...] = jnp.zeros_like(rows_acc)
        back_acc[...] = jnp.zeros_like(back_acc)

    w_in, w_out = win_ref[...], wout_ref[...]
    for r in row_chunks(x_ref.shape[0]):
        act, dpre = hidden_pair(x_ref[r, :], drows_ref[r, :], w_in, w_out)
        act_ref[r, :] = act
        dpre_ref[r, :] = dpre
        rows_acc[r, :] += dot(act, w_out)
        back_acc[r, :] += dot_nt(dpre, w_in)

    @pl.when(step == pl.num_programs(0) - 1)
    def _():
        for r in row_chunks(x_ref.shape[0]):
            rows = rows_acc[r, :].astype(jnp.bfloat16)
            rows_ref[r, :] = rows
            d_gate = jnp.sum(
                c_ref[r, :].astype(jnp.float32) * rows.astype(jnp.float32), axis=1, keepdims=True
            )
            p = probs[r, :]
            d_probs = pick * d_gate + aux_ref[0:1, :]
            d_log = p * (d_probs - jnp.sum(d_probs * p, axis=1, keepdims=True))
            d_log = d_log.astype(jnp.bfloat16)
            dlog_ref[r, :] = d_log
            back = back_acc[r, :].astype(jnp.bfloat16).astype(jnp.float32)
            back_ref[r, :] = (back + dot_nt(d_log, router_ref[...])).astype(jnp.bfloat16)


def whole(shape):
    return pl.BlockSpec(shape, lambda t: (0,) * len(shape))


def expert_pass(x, cot, router, pick, aux, w_in, w_out, experts):
    rows = x.shape[0]
    wide = jax.ShapeDtypeStruct((rows, FF), jnp.bfloat16)
    narrow = jax.ShapeDtypeStruct((rows, D), jnp.bfloat16)
    return pl.pallas_call(
        functools.partial(expert_kernel, experts),
        grid=(FF // TILE,),
        in_specs=[
            whole((rows, D)),
            whole((rows, D)),
            whole((D, SUB)),
            whole((8, SUB)),
            whole((8, SUB)),
            pl.BlockSpec((D, TILE), lambda t: (0, t)),
            pl.BlockSpec((TILE, D), lambda t: (t, 0)),
        ],
        out_specs=[
            whole((rows, D)),
            whole((rows, D)),
            pl.BlockSpec((rows, TILE), lambda t: (0, t)),
            pl.BlockSpec((rows, TILE), lambda t: (0, t)),
            whole((rows, D)),
            whole((rows, SUB)),
        ],
        out_shape=[narrow, narrow, wide, wide, narrow, jax.ShapeDtypeStruct((rows, SUB), jnp.bfloat16)],
        scratch_shapes=[
            pltpu.VMEM((rows, SUB), jnp.float32),
            pltpu.VMEM((rows, D), jnp.float32),
            pltpu.VMEM((rows, D), jnp.float32),
        ],
        compiler_params=pltpu.CompilerParams(
            dimension_semantics=("arbitrary",), vmem_limit_bytes=VMEM_LIMIT
        ),
        cost_estimate=pl.CostEstimate(
            flops=8 * rows * D * FF, bytes_accessed=30_000_000, transcendentals=rows * FF
        ),
    )(x, cot, router, pick, aux, w_in, w_out)


def transposed(target, source, place):
    for r in row_chunks(source.shape[0]):
        at = pl.multiple_of(place + r.start, QB)
        target[:, pl.ds(at, QB)] = source[r, :].T


def weight_kernel(experts, paired, *refs):
    if paired:
        (x_ref, drows_ref, act_ref, dpre_ref, rep_ref, x2_ref, c2_ref, router_ref, pick_ref, win_ref,
         wout_ref, din_ref, dout_ref, xt, dt, drows2, acts, dpres) = refs
        own = rep_ref[0] * x_ref.shape[0]
        other = x_ref.shape[0] - own
    else:
        x_ref, drows_ref, act_ref, dpre_ref, din_ref, dout_ref, xt, dt = refs
        own = 0

    @pl.when(pl.program_id(0) == 0)
    def _():
        transposed(xt, x_ref, own)
        transposed(dt, drows_ref, own)
        if paired:
            for r in row_chunks(x2_ref.shape[0]):
                _, gate = routing(x2_ref[r, :], router_ref[...], pick_ref[0:1, :], experts)
                drows2[r, :] = (gate * c2_ref[r, :].astype(jnp.float32)).astype(jnp.bfloat16)
            transposed(xt, x2_ref, other)
            transposed(dt, drows2, other)

    if paired:
        w_in, w_out = win_ref[...], wout_ref[...]
        for r in row_chunks(x2_ref.shape[0]):
            act, dpre = hidden_pair(x2_ref[r, :], drows2[r, :], w_in, w_out)
            at = pl.ds(pl.multiple_of(other + r.start, QB), QB)
            acts[at, :] = act
            dpres[at, :] = dpre
            at = pl.ds(pl.multiple_of(own + r.start, QB), QB)
            acts[at, :] = act_ref[r, :]
            dpres[at, :] = dpre_ref[r, :]
        act, dpre = acts[...], dpres[...]
    else:
        act, dpre = act_ref[...], dpre_ref[...]
    din_ref[...] = dot(xt[...], dpre)
    dout_ref[...] = dot(dt[...], act).T


def weight_pass(own, other, experts):
    x, drows, act, dpre = own
    rows = x.shape[0]
    paired = other is not None
    total = 2 * rows if paired else rows
    narrow, wide = whole((rows, D)), pl.BlockSpec((rows, TILE), lambda t: (0, t))
    in_specs = [narrow, narrow, wide, wide]
    scratch = [pltpu.VMEM((D, total), jnp.bfloat16)] * 2
    args = (x, drows, act, dpre)
    if paired:
        in_specs += [
            pl.BlockSpec(memory_space=pltpu.SMEM),
            narrow,
            narrow,
            whole((D, SUB)),
            whole((8, SUB)),
            pl.BlockSpec((D, TILE), lambda t: (0, t)),
            pl.BlockSpec((TILE, D), lambda t: (t, 0)),
        ]
        scratch += [
            pltpu.VMEM((rows, D), jnp.bfloat16),
            pltpu.VMEM((total, TILE), jnp.bfloat16),
            pltpu.VMEM((total, TILE), jnp.bfloat16),
        ]
        args += tuple(other)
    return pl.pallas_call(
        functools.partial(weight_kernel, experts, paired),
        grid=(FF // TILE,),
        in_specs=in_specs,
        out_specs=[
            pl.BlockSpec((D, TILE), lambda t: (0, t)),
            pl.BlockSpec((TILE, D), lambda t: (t, 0)),
        ],
        out_shape=[
            jax.ShapeDtypeStruct((D, FF), jnp.float32),
            jax.ShapeDtypeStruct((FF, D), jnp.float32),
        ],
        scratch_shapes=scratch,
        compiler_params=pltpu.CompilerParams(
            dimension_semantics=("arbitrary",), vmem_limit_bytes=VMEM_LIMIT
        ),
        cost_estimate=pl.CostEstimate(
            flops=(12 if paired else 4) * rows * D * FF,
            bytes_accessed=45_000_000,
            transcendentals=rows * FF if paired else 0,
        ),
    )(*args)


EPSILON = 1e-06
AUX_WEIGHT = 0.01
PRECISE = lax.Precision.HIGHEST
GROUP = ("shard", "seq")
EVERY = ("rep", "shard", "seq")


def exchange(x, axis, hop):
    count = lax.axis_size(axis)
    return lax.ppermute(x, axis, [(i, i ^ hop) for i in range(count)])


def bits_of(axis):
    return lax.axis_size(axis).bit_length() - 1


def bit_at(axis, bit):
    return (lax.axis_index(axis) >> bit) & 1


def both_halves(x, axis, bit, dim):
    other = exchange(x, axis, 1 << bit)
    size = x.shape[dim]
    rec = jnp.concatenate([other, x, other], axis=dim)
    return lax.dynamic_slice_in_dim(rec, (1 - bit_at(axis, bit)) * size, 2 * size, axis=dim)


def all_blocks(x, axis, dim):
    count = lax.axis_size(axis)
    size = x.shape[dim]
    turned = [
        lax.ppermute(x, axis, [(i, (i + k) % count) for i in range(count)])
        for k in range(count - 1, 0, -1)
    ]
    rec = jnp.concatenate(turned + [x] + turned, axis=dim)
    start = (count - 1 - lax.axis_index(axis)) * size
    return lax.dynamic_slice_in_dim(rec, start, count * size, axis=dim)


def gather_rows(x, parts):
    seq_bits = bits_of("seq")
    outs = []
    for turn, (start, stop) in enumerate(parts):
        y = x[:, start:stop].reshape((1,) * (1 + seq_bits) + (x.shape[0], stop - start))
        order = ["shard"] + list(range(seq_bits - 1, 0, -1))
        if turn % 2 == 1:
            order = order[::-1]
        for what in order + [0]:
            if what == "shard":
                y = all_blocks(y, "shard", 0)
            else:
                y = both_halves(y, "seq", what, seq_bits - what)
        outs.append(y.reshape(-1, stop - start))
    return outs


def half_kept(x, axis, bit, dim):
    size = x.shape[dim] // 2
    mine = bit_at(axis, bit)
    kept = lax.dynamic_slice_in_dim(x, mine * size, size, axis=dim)
    sent = lax.dynamic_slice_in_dim(x, (1 - mine) * size, size, axis=dim)
    got = exchange(sent, axis, 1 << bit)
    return (kept.astype(jnp.float32) + got.astype(jnp.float32)).astype(jnp.bfloat16)


def scatter_sums(x, parts):
    seq_bits, shard_bits = bits_of("seq"), bits_of("shard")
    rows = x.shape[0] >> (seq_bits + shard_bits)
    outs = []
    for turn, (start, stop) in enumerate(parts):
        y = x[:, start:stop].reshape((2,) * (shard_bits + seq_bits) + (rows, stop - start))
        far = [("shard", b) for b in range(shard_bits - 1, -1, -1)]
        near = [("seq", b) for b in range(seq_bits - 1, 0, -1)]
        order = near + far if turn % 2 == 0 else far + near
        for axis, bit in [("seq", 0)] + order:
            dim = shard_bits - 1 - bit if axis == "shard" else shard_bits + seq_bits - 1 - bit
            y = half_kept(y, axis, bit, dim)
        y = y.reshape(rows, stop - start)
        for bit in range(bits_of("rep")):
            total = y.astype(jnp.float32) + exchange(y, "rep", 1 << bit).astype(jnp.float32)
            y = total.astype(jnp.bfloat16)
        outs.append(total)
    return outs


def sum_everywhere(x):
    for axis in ("seq", "shard", "rep"):
        for bit in range(bits_of(axis)):
            x = x + exchange(x, axis, 1 << bit)
    return x


def rms_norm(vectors, gains):
    return (
        vectors * lax.rsqrt(jnp.mean(vectors * vectors, axis=-1, keepdims=True) + EPSILON) * gains
    )


def dot_tn(a, b):
    return lax.dot_general(a, b, (((0,), (0,)), ((), ())), preferred_element_type=jnp.float32)


def doc_index(places, doc_ends):
    return jnp.sum((places[:, None] >= doc_ends[None, :]).astype(jnp.int32), axis=1)


def wide_row(values):
    row = jnp.pad(values.astype(jnp.float32), (0, SUB - values.shape[0]))
    return jnp.broadcast_to(row[None, :], (8, SUB))


def routed_across(x):
    return lax.all_to_all(x, GROUP, split_axis=0, concat_axis=0, tiled=True)


def shards(
    tokens,
    doc_lengths,
    expert_ids,
    cotangent,
    gain_attn,
    gain_ffn,
    w_query,
    w_key,
    w_value,
    w_attn_out,
    rel_table,
    w_router,
    w_expert_in,
    w_expert_out,
):
    rows = tokens.shape[0]
    seq_count = lax.axis_size("seq")
    rep_count = lax.axis_size("rep")
    experts = lax.axis_size(GROUP)
    all_devices = lax.axis_size(EVERY)
    capacity = 5 * rows // (4 * experts)
    slots = experts * capacity
    shard_rows = w_query.shape[0]
    table_rows = rel_table.shape[0]
    w_in, w_out = w_expert_in[0], w_expert_out[0]

    up = [(i, i + 1) for i in range(seq_count - 1)]
    down = [(i + 1, i) for i in range(seq_count - 1)]
    token_span = jnp.concatenate(
        [lax.ppermute(tokens[rows - HALF :], "seq", up), tokens, lax.ppermute(tokens[:HALF], "seq", down)],
        axis=0,
    )
    small = jnp.concatenate(
        [
            w_router,
            gain_attn[:, None],
            gain_ffn[:, None],
            jnp.pad(rel_table, ((0, shard_rows - table_rows), (0, 0))),
        ],
        axis=1,
    )
    small = jnp.pad(small, ((0, 0), (0, SUB - small.shape[1])))
    first = jnp.concatenate([small, w_query, w_key, w_value], axis=1)
    cut = 10 * SUB
    left, right = gather_rows(first, [(0, cut), (cut, first.shape[1])])
    extra = left[:, :SUB]
    w_qkv = jnp.concatenate([left[:, SUB:], right], axis=1)
    router = extra[:, :experts]
    router_wide = jnp.pad(router, ((0, 0), (0, SUB - experts)))
    g_attn = extra[:, experts].astype(jnp.float32)
    g_ffn = extra[:, experts + 1].astype(jnp.float32)
    table = extra.reshape(experts, shard_rows, SUB)[:, :table_rows, experts + 2 : experts + 2 + HEADS]
    table = table.reshape(BUCKETS, HEADS).astype(jnp.float32)
    w_proj = jnp.concatenate(gather_rows(w_attn_out, [(0, 3 * SUB), (3 * SUB, D)]), axis=1)

    first_place = lax.axis_index("seq") * rows
    doc_ends = jnp.cumsum(doc_lengths[0])
    total_live = doc_ends[DOCS - 1]
    q_places = first_place + jnp.arange(rows, dtype=jnp.int32)
    k_places = first_place - HALF + jnp.arange(rows + 2 * HALF, dtype=jnp.int32)
    q_docs = doc_index(q_places, doc_ends)
    k_docs = doc_index(k_places, doc_ends)
    q_live = q_places < total_live
    k_live = (k_places >= 0) & (k_places < total_live)
    docs = jnp.arange(SUB, dtype=jnp.int32)[None, :]
    q_feat = ((q_docs[:, None] == docs) & (docs < DOCS)).astype(jnp.bfloat16)
    barred = (docs < DOCS) & ~((k_docs[:, None] == docs) & k_live[:, None])
    k_feat = jnp.where(barred, MASKED_SCORE, 0.0).astype(jnp.bfloat16)
    live = jnp.broadcast_to(q_live[:, None], (rows, SUB)).astype(jnp.bfloat16)
    chosen_ids = expert_ids[:, 0]
    chosen = (chosen_ids[:, None] == jnp.arange(experts, dtype=jnp.int32)[None, :]).astype(
        jnp.int32
    ) * q_live.astype(jnp.int32)[:, None]
    chosen_f = chosen.astype(jnp.float32)
    ranked = jnp.cumsum(chosen, axis=0)
    slot_index = jnp.sum(ranked * chosen, axis=1) - 1
    target = jnp.where(q_live, chosen_ids * capacity + slot_index, slots)
    hot = (target[None, :] == jnp.arange(slots, dtype=jnp.int32)[:, None]).astype(jnp.bfloat16)
    counts_all = sum_everywhere(jnp.sum(chosen_f, axis=0))
    live_all = jnp.sum(counts_all)
    shares = counts_all / live_all
    me = lax.axis_index(GROUP)
    pick = wide_row(jnp.arange(experts) == me)
    aux = wide_row((AUX_WEIGHT * experts / live_all) * shares)

    def to_experts(values):
        sent = dot(hot, values).astype(jnp.bfloat16)
        return routed_across(sent.reshape(experts, capacity, D)).reshape(slots, D)

    def from_experts(values):
        return dot_tn(hot, routed_across(values.reshape(experts, capacity, D)).reshape(slots, D))

    cot_rows = to_experts(cotangent)

    inputs = tokens.astype(jnp.float32)
    normed_span, span_pull = jax.vjp(rms_norm, token_span.astype(jnp.float32), g_attn)
    normed_span = normed_span.astype(jnp.bfloat16)
    normed_one = normed_span[HALF : HALF + rows]
    queries = dot(normed_one, w_qkv[:, :D]).astype(jnp.bfloat16)
    key_value = dot(normed_span, w_qkv[:, D:]).astype(jnp.bfloat16)
    bias_rows = jnp.einsum("rxb,bh->hrx", one_hot(bias_buckets()), table, precision=PRECISE)
    context, expo, inverse = attention_forward(queries, key_value, q_feat, k_feat, live, bias_rows)
    hidden_state = inputs + dot(context, w_proj)

    ffn_normed, ffn_pull = jax.vjp(rms_norm, hidden_state, g_ffn)
    normed_two = ffn_normed.astype(jnp.bfloat16)
    x_rows = to_experts(normed_two)
    out_rows, back_rows, act, d_pre, d_rows, d_logits = expert_pass(
        x_rows, cot_rows, router_wide, pick, aux, w_in, w_out, experts
    )
    d_normed_two = from_experts(back_rows)
    expert_rows = from_experts(out_rows)
    d_router = dot_tn(x_rows, d_logits)[:, :experts]
    own = (x_rows, d_rows, act, d_pre)
    if rep_count == 2:
        order = lax.axis_index("rep").reshape(1)
        x_other, cot_other = exchange(x_rows, "rep", 1), exchange(cot_rows, "rep", 1)
        other = (order, x_other, cot_other, router_wide, pick, w_in, w_out)
        d_expert_in, d_expert_out = weight_pass(own, other, experts)
    else:
        d_expert_in, d_expert_out = (
            lax.psum(g.astype(jnp.bfloat16), "rep").astype(jnp.float32)
            for g in weight_pass(own, None, experts)
        )

    router_probs = jax.nn.softmax(dot(normed_two, router), axis=-1)
    gating = jnp.sum(router_probs * chosen_f, axis=1)
    mass_all = sum_everywhere(jnp.sum(router_probs * q_live.astype(jnp.float32)[:, None], axis=0))
    balance = experts * jnp.sum(shares * mass_all) / live_all
    importance = experts * mass_all / (rows * all_devices)
    mixed = (hidden_state + gating[:, None] * expert_rows).astype(jnp.bfloat16)

    hidden_back, d_gain_ffn = ffn_pull(d_normed_two)
    d_hidden = cotangent.astype(jnp.float32) + hidden_back
    d_attn = d_hidden.astype(jnp.bfloat16)
    d_context = dot_nt(d_attn, w_proj).astype(jnp.bfloat16)
    d_attn_out = dot_tn(context, d_attn)
    more = jnp.concatenate([d_router, d_gain_ffn[:, None]], axis=1)
    more = jnp.pad(more, ((0, 0), (0, SUB - more.shape[1])))
    early = jnp.concatenate([d_attn_out, more], axis=1).astype(jnp.bfloat16)
    early_cut = 4 * SUB
    early = jnp.concatenate(scatter_sums(early, [(0, early_cut), (early_cut, D + SUB)]), axis=1)

    pieces, sums, d_bias = [], [], []
    for pairs in (range(0, 3), range(3, 6)):
        d_q, d_k, d_v, d_b = attention_backward(
            queries, key_value, live, expo, inverse, context, d_context, pairs[0], len(pairs)
        )
        pieces.append((d_q, d_k, d_v))
        d_bias.append(d_b)
        grads = jnp.concatenate(
            [
                dot_tn(normed_one, d_q).astype(jnp.bfloat16),
                dot_tn(normed_span, d_k).astype(jnp.bfloat16),
                dot_tn(normed_span, d_v).astype(jnp.bfloat16),
            ],
            axis=1,
        )
        width = grads.shape[1]
        half = width // (2 * SUB) * SUB
        summed = jnp.concatenate(scatter_sums(grads, [(0, half), (half, width)]), axis=1)
        sums.append(jnp.split(summed, 3, axis=1))
    d_query, d_key, d_value = (jnp.concatenate(s, axis=1) for s in zip(*sums))
    d_q, d_k, d_v = (jnp.concatenate(s, axis=1) for s in zip(*pieces))
    d_span = dot_nt(jnp.concatenate([d_k, d_v], axis=1), w_qkv[:, D:])
    d_span = jnp.concatenate(
        [d_span[:HALF], d_span[HALF : HALF + rows] + dot_nt(d_q, w_qkv[:, :D]), d_span[HALF + rows :]],
        axis=0,
    )
    from_above = lax.ppermute(d_span[:HALF].astype(jnp.bfloat16), "seq", down)
    from_below = lax.ppermute(d_span[HALF + rows :].astype(jnp.bfloat16), "seq", up)
    gap = jnp.zeros((rows - HALF, D), jnp.float32)
    d_normed_one = (
        d_span[HALF : HALF + rows]
        + jnp.concatenate([from_below.astype(jnp.float32), gap], axis=0)
        + jnp.concatenate([gap, from_above.astype(jnp.float32)], axis=0)
    )
    _, attn_pull = jax.vjp(lambda v: rms_norm(v, g_attn), inputs)
    d_tokens = d_hidden + attn_pull(d_normed_one)[0]
    d_gain_attn = span_pull(d_span)[1]
    d_table = jnp.einsum(
        "hrx,rxb->bh", jnp.concatenate(d_bias, axis=0), one_hot(grad_buckets()), precision=PRECISE
    )
    d_table = jnp.pad(
        d_table.reshape(experts, table_rows, HEADS), ((0, 0), (0, shard_rows - table_rows), (0, 0))
    ).reshape(D, HEADS)
    late = jnp.concatenate([d_gain_attn[:, None], d_table], axis=1).astype(jnp.bfloat16)
    late = jnp.pad(late, ((0, 0), (0, SUB - late.shape[1])))
    late = scatter_sums(late, [(0, SUB)])[0]
    return (
        mixed,
        balance,
        importance,
        d_tokens,
        late[:, 0],
        early[:, D + experts],
        d_query,
        d_key,
        d_value,
        early[:, :D],
        late[:table_rows, 1 : 1 + HEADS],
        early[:, D : D + experts],
        d_expert_in[None],
        d_expert_out[None],
    )


def solution(mesh):
    split = P(EVERY, None)
    shared = P(GROUP, None)
    gains = P(GROUP)
    stacked = P(GROUP, None, None)
    weights = (shared,) * 6 + (stacked,) * 2
    return jax.shard_map(
        shards,
        mesh=mesh,
        in_specs=(split, P(("rep", "shard"), None), split, split, gains, gains) + weights,
        out_specs=(split, P(), P(), split, gains, gains) + weights,
        check_vma=False,
    )
```

```python
import functools
import math

import jax
import jax.numpy as jnp
import numpy as np
from jax import lax
from jax.experimental import pallas as pl
from jax.experimental.pallas import tpu as pltpu
from jax.sharding import PartitionSpec as P

D = 768
HEADS = 12
HEAD = 64
BUCKETS = 32
MAXDIST = 128
WINDOW = 1024
DOCS = 4
MASKED_SCORE = -1e30
HALF = WINDOW // 2
QB = 256
SUB = 128
KB = QB + WINDOW
PAIRS = HEADS // 2
VMEM_LIMIT = 56 * 1024 * 1024


def thresholds(max_distance, half_count):
    exact_span = half_count // 2
    collected = list(range(1, exact_span + 1))
    for target_level in range(exact_span + 1, half_count):
        candidate = exact_span
        while (
            exact_span
            + int(
                math.log(candidate / exact_span)
                / math.log(max_distance / exact_span)
                * (half_count - exact_span)
            )
            < target_level
        ):
            candidate += 1
        collected.append(candidate)
    return collected


LIMITS = thresholds(MAXDIST, BUCKETS // 2)
assert LIMITS[-1] <= SUB


def bucket_table(distance):
    distance = np.asarray(distance)
    magnitude = np.abs(distance)
    bucket_id = (distance > 0).astype(np.int32) * (BUCKETS // 2)
    for boundary in LIMITS:
        bucket_id = bucket_id + (magnitude >= boundary)
    return bucket_id


def bias_buckets():
    lane = np.arange(2 * SUB)
    rows = []
    for m in (-1, 0, 1):
        rows.append(bucket_table(SUB * m - lane + np.where(lane >= SUB, 2 * SUB, 0)))
    rows.append(np.full(2 * SUB, bucket_table(-WINDOW)))
    rows.append(np.full(2 * SUB, bucket_table(WINDOW)))
    rows += [np.zeros(2 * SUB, np.int32)] * 3
    return np.stack(rows)


def grad_buckets():
    lane = np.arange(SUB)
    rows = [bucket_table(SUB * m - lane) for m in (-1, 0, 1)]
    rows += [bucket_table(SUB * (m + 1) - lane) for m in (-1, 0, 1)]
    rows.append(np.full(SUB, bucket_table(-WINDOW)))
    rows.append(np.full(SUB, bucket_table(WINDOW)))
    return np.stack(rows)


def one_hot(ids):
    return (ids[..., None] == np.arange(BUCKETS)).astype(np.float32)


def dot(a, b):
    return jnp.dot(a, b, preferred_element_type=jnp.float32)


def dot_nt(a, b):
    return lax.dot_general(a, b, (((1,), (1,)), ((), ())), preferred_element_type=jnp.float32)


def head_lanes(shape, axis, h):
    place = lax.broadcasted_iota(jnp.int32, shape, axis)
    return (place < HEAD) if h == 0 else (place >= HEAD)


def fold8(x, op):
    return op(x.reshape(x.shape[0] // 8, 8, x.shape[1]), axis=0)


def block_kind(a, b):
    m = a - b - 4
    return m, "n" if m < -1 else "p" if m > 1 else "v"


def forward_kernel(
    q_ref,
    k_ref,
    v_ref,
    qf_ref,
    kf_ref,
    live_ref,
    w_ref,
    ctx_ref,
    e_ref,
    inv_ref,
    vt,
    bias,
    s_ref,
    peak_ref,
):
    steps = q_ref.shape[0] // QB
    for h in range(2):
        for m in range(3):
            row = jnp.broadcast_to(w_ref[h, m : m + 1, :], (SUB, 2 * SUB))
            bias[h, m] = pltpu.roll(row, 0, 1, stride=1, stride_axis=0)[:, :SUB]
    for s in range(v_ref.shape[0] // QB):
        vt[:, s * QB : (s + 1) * QB] = v_ref[s * QB : (s + 1) * QB, :].T
    row_id = lax.broadcasted_iota(jnp.int32, (SUB, SUB), 0)
    col_id = lax.broadcasted_iota(jnp.int32, (SUB, SUB), 1)

    def stage(score, weigh):
        if score is not None:
            s_now, p_now = s_ref.at[score % 2], peak_ref.at[score % 2]
            rows = pl.ds(pl.multiple_of(score * QB, QB), QB)
            q, qf = q_ref[rows, :], qf_ref[rows, :]
            qx = [
                jnp.concatenate([jnp.where(head_lanes(q.shape, 1, h), q, 0), qf], axis=1)
                for h in range(2)
            ]
            tops = {}
        if weigh is not None:
            s_then, p_then = s_ref.at[weigh % 2], peak_ref.at[weigh % 2]
            totals = {(h, b): jnp.zeros((8, SUB), jnp.float32) for h in range(2) for b in range(2)}
            ct = [jnp.zeros((HEAD, QB), jnp.float32)] * 2
        for c in range(KB // QB):
            if score is not None:
                place = pl.ds(pl.multiple_of(score * QB + c * QB, QB), QB)
                kx = jnp.concatenate([k_ref[place, :], kf_ref[place, :]], axis=1)
                scores = [dot_nt(kx, qx[h]) for h in range(2)]
            if weigh is not None:
                place = pl.ds(pl.multiple_of(weigh * QB + c * QB, QB), QB)
                for h in range(2):
                    chunk = []
                    for a in range(2 * c, 2 * c + 2):
                        line = []
                        for b in range(2):
                            m, kind = block_kind(a, b)
                            if abs(m) > 4:
                                line.append(jnp.zeros((SUB, SUB), jnp.bfloat16))
                                continue
                            row = 3 * h + "nvp".index(kind)
                            cols = slice(b * SUB, (b + 1) * SUB)
                            e = jnp.exp(
                                s_then[h, a * SUB : (a + 1) * SUB, cols] - p_then[row : row + 1, cols]
                            )
                            totals[h, b] = totals[h, b] + fold8(e, jnp.sum)
                            line.append(e.astype(jnp.bfloat16))
                        chunk.append(jnp.concatenate(line, axis=1))
                    chunk = jnp.concatenate(chunk, axis=0)
                    e_ref[0, weigh, h, c * QB : (c + 1) * QB, :] = chunk
                    ct[h] = ct[h] + dot(vt[h * HEAD : (h + 1) * HEAD, place], chunk)
            if score is None:
                continue
            for h in range(2):
                for a in range(2 * c, 2 * c + 2):
                    for b in range(2):
                        m, kind = block_kind(a, b)
                        if abs(m) > 4:
                            continue
                        x = scores[h][
                            (a - 2 * c) * SUB : (a - 2 * c + 1) * SUB, b * SUB : (b + 1) * SUB
                        ]
                        if m == -4:
                            x = jnp.where(row_id >= col_id, x, MASKED_SCORE)
                        if m == 4:
                            x = jnp.where(row_id <= col_id, x, MASKED_SCORE)
                        if kind == "v":
                            x = x + bias[h, m + 1]
                        s_now[h, a * SUB : (a + 1) * SUB, b * SUB : (b + 1) * SUB] = x
                        top = fold8(x, jnp.max)
                        old = tops.get((h, b, kind))
                        tops[h, b, kind] = top if old is None else jnp.maximum(old, top)
        if score is not None:
            for h in range(2):
                neg, pos = w_ref[h, 3:4, :SUB], w_ref[h, 4:5, :SUB]
                for b in range(2):
                    peak = jnp.maximum(
                        jnp.maximum(tops[h, b, "n"] + neg, tops[h, b, "p"] + pos), tops[h, b, "v"]
                    )
                    peak = jnp.max(peak, axis=0, keepdims=True)
                    p_now[3 * h : 3 * h + 3, b * SUB : (b + 1) * SUB] = jnp.concatenate(
                        [peak - neg, peak, peak - pos], axis=0
                    )
        if weigh is not None:
            contexts = []
            for h in range(2):
                total = [jnp.sum(totals[h, b], axis=0, keepdims=True) for b in range(2)]
                inv = 1.0 / jnp.concatenate(total, axis=1)
                inv_ref[0, weigh, h : h + 1, :] = inv
                contexts.append(ct[h] * inv)
            context = jnp.concatenate(contexts, axis=0).T.astype(jnp.bfloat16)
            rows = pl.ds(pl.multiple_of(weigh * QB, QB), QB)
            own = v_ref[pl.ds(pl.multiple_of(weigh * QB + HALF, QB), QB), :]
            ctx_ref[rows, :] = jnp.where(live_ref[rows, :] > 0, context, own)

    stage(0, None)

    def both(t, _):
        stage(t, t - 1)
        return 0

    lax.fori_loop(1, steps, both, 0)
    stage(None, steps - 1)


def backward_kernel(
    q_ref,
    k_ref,
    v_ref,
    live_ref,
    e_ref,
    inv_ref,
    ctx_ref,
    dctx_ref,
    dq_ref,
    dk_ref,
    dv_ref,
    db_ref,
    kt,
    dk_acc,
    dv_acc,
    acc,
    far,
):
    steps = q_ref.shape[0] // QB
    for s in range(k_ref.shape[0] // QB):
        kt[:, s * QB : (s + 1) * QB] = k_ref[s * QB : (s + 1) * QB, :].T
    dk_acc[...] = jnp.zeros_like(dk_acc)
    dv_acc[...] = jnp.zeros_like(dv_acc)
    acc[...] = jnp.zeros_like(acc)
    far[...] = jnp.zeros_like(far)

    def block(i, _):
        rows = pl.ds(pl.multiple_of(i * QB, QB), QB)
        q = q_ref[rows, :]
        dctx = dctx_ref[rows, :].astype(jnp.float32)
        kept = jnp.where(live_ref[rows, :] > 0, dctx, 0.0)
        prod = (kept * ctx_ref[rows, :].astype(jnp.float32)).T
        kept_t = kept.T
        qs, dts, deltas = [], [], []
        for h in range(2):
            inv = inv_ref[0, i, h : h + 1, :]
            qs.append(jnp.where(head_lanes(q.shape, 1, h), q, 0))
            dts.append(
                jnp.where(head_lanes(kept_t.shape, 0, h), kept_t * inv, 0.0).astype(jnp.bfloat16)
            )
            deltas.append(jnp.sum(prod[h * HEAD : (h + 1) * HEAD], axis=0, keepdims=True) * inv)
        q_both = jnp.concatenate(qs, axis=0)
        dt_both = jnp.concatenate(dts, axis=1)
        fars = [[jnp.zeros((8, SUB), jnp.float32)] * 2 for _ in range(2)]
        dqt = [jnp.zeros((HEAD, QB), jnp.float32)] * 2

        def places(c):
            return pl.ds(pl.multiple_of(i * QB + c * QB, QB), QB)

        def products(c):
            vc = v_ref[places(c), :]
            return [dot(vc, dts[h]) for h in range(2)]

        ahead = products(0)
        for c in range(KB // QB):
            place = places(c)
            dps = ahead
            if c + 1 < KB // QB:
                ahead = products(c + 1)
            grads, weights = [], []
            for h in range(2):
                e = e_ref[0, i, h, c * QB : (c + 1) * QB, :]
                ds = e.astype(jnp.float32) * (dps[h] - deltas[h])
                for a in range(2 * c, 2 * c + 2):
                    for b in range(2):
                        m, kind = block_kind(a, b)
                        x = ds[(a - 2 * c) * SUB : (a - 2 * c + 1) * SUB, b * SUB : (b + 1) * SUB]
                        if abs(m) > 4:
                            continue
                        if kind == "v":
                            acc[h, m + 1] += x
                        else:
                            side = "np".index(kind)
                            fars[h][side] = fars[h][side] + fold8(x, jnp.sum)
                ds = ds.astype(jnp.bfloat16)
                dqt[h] = dqt[h] + dot(kt[h * HEAD : (h + 1) * HEAD, place], ds)
                grads.append(ds)
                weights.append(e)
            dk_acc[place, :] += dot(jnp.concatenate(grads, axis=1), q_both)
            dv_acc[place, :] += dot_nt(jnp.concatenate(weights, axis=1), dt_both)
        dq_ref[rows, :] = jnp.concatenate(dqt, axis=0).T.astype(jnp.bfloat16)
        own = pl.ds(pl.multiple_of(i * QB + HALF, QB), QB)
        dv_acc[own, :] += dctx - kept
        for h in range(2):
            for side in range(2):
                far[h, side] += fars[h][side]
        return 0

    lax.fori_loop(0, steps, block, 0)
    dk_ref[...] = dk_acc[...].astype(jnp.bfloat16)
    dv_ref[...] = dv_acc[...].astype(jnp.bfloat16)
    row_id = lax.broadcasted_iota(jnp.int32, (SUB, SUB), 0)
    col_id = lax.broadcasted_iota(jnp.int32, (SUB, SUB), 1)
    sublane = lax.broadcasted_iota(jnp.int32, (8, SUB), 0)
    for h in range(2):
        sums = []
        for upper in (True, False):
            for m in range(3):
                x = jnp.where((col_id >= row_id) == upper, acc[h, m], 0.0)
                y = x[:8]
                for g in range(1, SUB // 8):
                    y = y + pltpu.roll(x[8 * g : 8 * g + 8], SUB - 8 * g, 1)
                for bit in range(3):
                    y = jnp.where(
                        (sublane >> bit) % 2 == 1, pltpu.roll(y, SUB - (1 << bit), 1), y
                    )
                sums.append(jnp.sum(y, axis=0, keepdims=True))
        for side in range(2):
            sums.append(jnp.sum(far[h, side], axis=0, keepdims=True))
        db_ref[h] = jnp.concatenate(sums, axis=0)


def spec(shape, index):
    return pl.BlockSpec(shape, index)


def attention_forward(queries, keys, values, q_feat, k_feat, live, bias_rows):
    rows, span = queries.shape[0], keys.shape[0]
    steps = rows // QB
    return pl.pallas_call(
        forward_kernel,
        grid=(PAIRS,),
        in_specs=[
            spec((rows, SUB), lambda p: (0, p)),
            spec((span, SUB), lambda p: (0, p)),
            spec((span, SUB), lambda p: (0, p)),
            spec((rows, SUB), lambda p: (0, 0)),
            spec((span, SUB), lambda p: (0, 0)),
            spec((rows, SUB), lambda p: (0, 0)),
            spec((2, 8, 2 * SUB), lambda p: (p, 0, 0)),
        ],
        out_specs=[
            spec((rows, SUB), lambda p: (0, p)),
            spec((1, steps, 2, KB, QB), lambda p: (p, 0, 0, 0, 0)),
            spec((1, steps, 8, QB), lambda p: (p, 0, 0, 0)),
        ],
        out_shape=[
            jax.ShapeDtypeStruct((rows, D), jnp.bfloat16),
            jax.ShapeDtypeStruct((PAIRS, steps, 2, KB, QB), jnp.bfloat16),
            jax.ShapeDtypeStruct((PAIRS, steps, 8, QB), jnp.float32),
        ],
        scratch_shapes=[
            pltpu.VMEM((SUB, span), jnp.bfloat16),
            pltpu.VMEM((2, 3, SUB, SUB), jnp.float32),
            pltpu.VMEM((2, 2, KB, QB), jnp.float32),
            pltpu.VMEM((2, 8, QB), jnp.float32),
        ],
        compiler_params=pltpu.CompilerParams(
            dimension_semantics=("arbitrary",), vmem_limit_bytes=VMEM_LIMIT
        ),
        cost_estimate=pl.CostEstimate(
            flops=4 * rows * KB * D * 4, bytes_accessed=45_000_000, transcendentals=rows * KB * HEADS
        ),
    )(queries, keys, values, q_feat, k_feat, live, bias_rows)


def attention_backward(
    queries, keys, values, live, expo, inverse, context, d_context, first, pairs
):
    rows, span = queries.shape[0], keys.shape[0]
    steps = rows // QB
    return pl.pallas_call(
        backward_kernel,
        grid=(pairs,),
        in_specs=[
            spec((rows, SUB), lambda p: (0, p + first)),
            spec((span, SUB), lambda p: (0, p + first)),
            spec((span, SUB), lambda p: (0, p + first)),
            spec((rows, SUB), lambda p: (0, 0)),
            spec((1, steps, 2, KB, QB), lambda p: (p + first, 0, 0, 0, 0)),
            spec((1, steps, 8, QB), lambda p: (p + first, 0, 0, 0)),
            spec((rows, SUB), lambda p: (0, p + first)),
            spec((rows, SUB), lambda p: (0, p + first)),
        ],
        out_specs=[
            spec((rows, SUB), lambda p: (0, p)),
            spec((span, SUB), lambda p: (0, p)),
            spec((span, SUB), lambda p: (0, p)),
            spec((2, 8, SUB), lambda p: (p, 0, 0)),
        ],
        out_shape=[
            jax.ShapeDtypeStruct((rows, pairs * SUB), jnp.bfloat16),
            jax.ShapeDtypeStruct((span, pairs * SUB), jnp.bfloat16),
            jax.ShapeDtypeStruct((span, pairs * SUB), jnp.bfloat16),
            jax.ShapeDtypeStruct((2 * pairs, 8, SUB), jnp.float32),
        ],
        scratch_shapes=[
            pltpu.VMEM((SUB, span), jnp.bfloat16),
            pltpu.VMEM((span, SUB), jnp.float32),
            pltpu.VMEM((span, SUB), jnp.float32),
            pltpu.VMEM((2, 3, SUB, SUB), jnp.float32),
            pltpu.VMEM((2, 2, 8, SUB), jnp.float32),
        ],
        compiler_params=pltpu.CompilerParams(
            dimension_semantics=("arbitrary",), vmem_limit_bytes=VMEM_LIMIT
        ),
        cost_estimate=pl.CostEstimate(
            flops=8 * rows * KB * pairs * SUB * 4, bytes_accessed=9_000_000 * pairs, transcendentals=0
        ),
    )(queries, keys, values, live, expo, inverse, context, d_context)


FF = 3072
TILE = 768
CHUNK = 768
WTILE = 512
WCHUNK = 256


def gelu_parts(v):
    scale = 0.7978845608
    square = v * v
    t = jnp.tanh(scale * v * (1.0 + 0.044715 * square))
    half = 0.5 * (1.0 + t)
    slope = half + 0.5 * v * (1.0 - t * t) * (scale + (3 * 0.044715 * scale) * square)
    return half * v, slope


def routing(x, router, pick, experts):
    logits = dot(x, router)
    lane = lax.broadcasted_iota(jnp.int32, logits.shape, 1)
    logits = jnp.where(lane < experts, logits, MASKED_SCORE)
    expo = jnp.exp(logits - jnp.max(logits, axis=1, keepdims=True))
    probs = expo / jnp.sum(expo, axis=1, keepdims=True)
    return probs, jnp.sum(probs * pick, axis=1, keepdims=True)


def hidden_pair(x, d_rows, w_in, w_out):
    inner, slope = gelu_parts(dot(x, w_in))
    d_pre = dot_nt(d_rows, w_out) * slope
    return inner.astype(jnp.bfloat16), d_pre.astype(jnp.bfloat16)


def row_chunks(rows, size=QB):
    return [slice(s, min(s + size, rows)) for s in range(0, rows, size)]


def expert_kernel(
    experts,
    x_ref,
    c_ref,
    router_ref,
    pick_ref,
    aux_ref,
    win_ref,
    wout_ref,
    rows_ref,
    back_ref,
    act_ref,
    dpre_ref,
    drows_ref,
    dlog_ref,
    probs,
    rows_acc,
    back_acc,
):
    step = pl.program_id(0)
    pick = pick_ref[0:1, :]

    @pl.when(step == 0)
    def _():
        for r in row_chunks(x_ref.shape[0]):
            p, gate = routing(x_ref[r, :], router_ref[...], pick, experts)
            probs[r, :] = p
            drows_ref[r, :] = (gate * c_ref[r, :].astype(jnp.float32)).astype(jnp.bfloat16)
        rows_acc[...] = jnp.zeros_like(rows_acc)
        back_acc[...] = jnp.zeros_like(back_acc)

    w_in, w_out = win_ref[...], wout_ref[...]
    for r in row_chunks(x_ref.shape[0], CHUNK):
        act, dpre = hidden_pair(x_ref[r, :], drows_ref[r, :], w_in, w_out)
        act_ref[r, :] = act
        dpre_ref[r, :] = dpre
        rows_acc[r, :] += dot(act, w_out)
        back_acc[r, :] += dot_nt(dpre, w_in)

    @pl.when(step == pl.num_programs(0) - 1)
    def _():
        for r in row_chunks(x_ref.shape[0]):
            rows = rows_acc[r, :].astype(jnp.bfloat16)
            rows_ref[r, :] = rows
            d_gate = jnp.sum(
                c_ref[r, :].astype(jnp.float32) * rows.astype(jnp.float32), axis=1, keepdims=True
            )
            p = probs[r, :]
            d_probs = pick * d_gate + aux_ref[0:1, :]
            d_log = p * (d_probs - jnp.sum(d_probs * p, axis=1, keepdims=True))
            d_log = d_log.astype(jnp.bfloat16)
            dlog_ref[r, :] = d_log
            back = back_acc[r, :].astype(jnp.bfloat16).astype(jnp.float32)
            back_ref[r, :] = (back + dot_nt(d_log, router_ref[...])).astype(jnp.bfloat16)


def whole(shape):
    return pl.BlockSpec(shape, lambda t: (0,) * len(shape))


def expert_pass(x, cot, router, pick, aux, w_in, w_out, experts):
    rows = x.shape[0]
    wide = jax.ShapeDtypeStruct((rows, FF), jnp.bfloat16)
    narrow = jax.ShapeDtypeStruct((rows, D), jnp.bfloat16)
    return pl.pallas_call(
        functools.partial(expert_kernel, experts),
        grid=(FF // TILE,),
        in_specs=[
            whole((rows, D)),
            whole((rows, D)),
            whole((D, SUB)),
            whole((8, SUB)),
            whole((8, SUB)),
            pl.BlockSpec((D, TILE), lambda t: (0, t)),
            pl.BlockSpec((TILE, D), lambda t: (t, 0)),
        ],
        out_specs=[
            whole((rows, D)),
            whole((rows, D)),
            pl.BlockSpec((rows, TILE), lambda t: (0, t)),
            pl.BlockSpec((rows, TILE), lambda t: (0, t)),
            whole((rows, D)),
            whole((rows, SUB)),
        ],
        out_shape=[narrow, narrow, wide, wide, narrow, jax.ShapeDtypeStruct((rows, SUB), jnp.bfloat16)],
        scratch_shapes=[
            pltpu.VMEM((rows, SUB), jnp.float32),
            pltpu.VMEM((rows, D), jnp.float32),
            pltpu.VMEM((rows, D), jnp.float32),
        ],
        compiler_params=pltpu.CompilerParams(
            dimension_semantics=("arbitrary",), vmem_limit_bytes=VMEM_LIMIT
        ),
        cost_estimate=pl.CostEstimate(
            flops=8 * rows * D * FF, bytes_accessed=30_000_000, transcendentals=rows * FF
        ),
    )(x, cot, router, pick, aux, w_in, w_out)


def transposed(target, source, place):
    for r in row_chunks(source.shape[0]):
        at = pl.multiple_of(place + r.start, QB)
        target[:, pl.ds(at, QB)] = source[r, :].T


def hidden_kernel(experts, x_ref, c_ref, router_ref, pick_ref, win_ref, wout_ref, act_ref, dpre_ref, drows_ref):
    @pl.when(pl.program_id(0) == 0)
    def _():
        for r in row_chunks(x_ref.shape[0]):
            _, gate = routing(x_ref[r, :], router_ref[...], pick_ref[0:1, :], experts)
            drows_ref[r, :] = (gate * c_ref[r, :].astype(jnp.float32)).astype(jnp.bfloat16)

    act, dpre = hidden_pair(x_ref[...], drows_ref[...], win_ref[...], wout_ref[...])
    act_ref[...] = act
    dpre_ref[...] = dpre


def hidden_pass(x, cot, router, pick, w_in, w_out, experts):
    rows = x.shape[0]
    wide = jax.ShapeDtypeStruct((rows, FF), jnp.bfloat16)
    wide_spec = pl.BlockSpec((rows, TILE), lambda t: (0, t))
    return pl.pallas_call(
        functools.partial(hidden_kernel, experts),
        grid=(FF // TILE,),
        in_specs=[
            whole((rows, D)),
            whole((rows, D)),
            whole((D, SUB)),
            whole((8, SUB)),
            pl.BlockSpec((D, TILE), lambda t: (0, t)),
            pl.BlockSpec((TILE, D), lambda t: (t, 0)),
        ],
        out_specs=[wide_spec, wide_spec, whole((rows, D))],
        out_shape=[wide, wide, jax.ShapeDtypeStruct((rows, D), jnp.bfloat16)],
        compiler_params=pltpu.CompilerParams(
            dimension_semantics=("arbitrary",), vmem_limit_bytes=VMEM_LIMIT
        ),
        cost_estimate=pl.CostEstimate(
            flops=4 * rows * D * FF, bytes_accessed=30_000_000, transcendentals=rows * FF
        ),
    )(x, cot, router, pick, w_in, w_out)


def weight_kernel(parts, more_ref, *refs):
    x_refs, drows_refs, act_refs, dpre_refs = (refs[k * parts : (k + 1) * parts] for k in range(4))
    din_old, dout_old, din_ref, dout_ref, xt, d_rows, act_t, dpres = refs[4 * parts :]
    sizes = [x.shape[0] for x in x_refs]
    starts = [sum(sizes[:k]) for k in range(parts)]

    @pl.when(pl.program_id(0) == 0)
    def _():
        for k in range(parts):
            transposed(xt, x_refs[k], starts[k])
            d_rows[starts[k] : starts[k] + sizes[k], :] = drows_refs[k][...]

    for k in range(parts):
        transposed(act_t, act_refs[k], starts[k])
        dpres[starts[k] : starts[k] + sizes[k], :] = dpre_refs[k][...]
    din_ref[...] = dot(xt[...], dpres[...])
    dout_ref[...] = dot(act_t[...], d_rows[...])

    @pl.when(more_ref[0] > 0)
    def _():
        din_ref[...] = din_ref[...] + din_old[...]
        dout_ref[...] = dout_ref[...] + dout_old[...]


def weight_pass(rows_of, old, more):
    sizes = [x.shape[0] for x in rows_of[0]]
    total = sum(sizes)
    narrow = [pl.BlockSpec((rows, D), lambda t, m: (0, 0)) for rows in sizes]
    wide = [pl.BlockSpec((rows, WTILE), lambda t, m: (0, t)) for rows in sizes]
    old_specs = [
        pl.BlockSpec((D, WTILE), lambda t, m: (0, t * m[0])),
        pl.BlockSpec((WTILE, D), lambda t, m: (t * m[0], 0)),
    ]
    new_specs = [
        pl.BlockSpec((D, WTILE), lambda t, m: (0, t)),
        pl.BlockSpec((WTILE, D), lambda t, m: (t, 0)),
    ]
    return pl.pallas_call(
        functools.partial(weight_kernel, len(sizes)),
        grid_spec=pltpu.PrefetchScalarGridSpec(
            num_scalar_prefetch=1,
            grid=(FF // WTILE,),
            in_specs=narrow * 2 + wide * 2 + old_specs,
            out_specs=new_specs,
            scratch_shapes=[
                pltpu.VMEM((D, total), jnp.bfloat16),
                pltpu.VMEM((total, D), jnp.bfloat16),
                pltpu.VMEM((WTILE, total), jnp.bfloat16),
                pltpu.VMEM((total, WTILE), jnp.bfloat16),
            ],
        ),
        out_shape=[
            jax.ShapeDtypeStruct((D, FF), jnp.float32),
            jax.ShapeDtypeStruct((FF, D), jnp.float32),
        ],
        compiler_params=pltpu.CompilerParams(
            dimension_semantics=("arbitrary",), vmem_limit_bytes=VMEM_LIMIT
        ),
        cost_estimate=pl.CostEstimate(
            flops=4 * total * D * FF, bytes_accessed=50_000_000, transcendentals=0
        ),
    )(jnp.full((1,), more, jnp.int32), *[array for group in rows_of for array in group], *old)


EPSILON = 1e-06
AUX_WEIGHT = 0.01
PRECISE = lax.Precision.HIGHEST
GROUP = ("shard", "seq")
EVERY = ("rep", "shard", "seq")


def exchange(x, axis, hop):
    count = lax.axis_size(axis)
    return lax.ppermute(x, axis, [(i, i ^ hop) for i in range(count)])


def bits_of(axis):
    return lax.axis_size(axis).bit_length() - 1


def bit_at(axis, bit):
    return (lax.axis_index(axis) >> bit) & 1


def both_halves(x, axis, bit, dim):
    other = exchange(x, axis, 1 << bit)
    size = x.shape[dim]
    rec = jnp.concatenate([other, x, other], axis=dim)
    return lax.dynamic_slice_in_dim(rec, (1 - bit_at(axis, bit)) * size, 2 * size, axis=dim)


def all_blocks(x, axis, dim):
    count = lax.axis_size(axis)
    size = x.shape[dim]
    turned = [
        lax.ppermute(x, axis, [(i, (i + k) % count) for i in range(count)])
        for k in range(count - 1, 0, -1)
    ]
    rec = jnp.concatenate(turned + [x] + turned, axis=dim)
    start = (count - 1 - lax.axis_index(axis)) * size
    return lax.dynamic_slice_in_dim(rec, start, count * size, axis=dim)


def gather_rows(parts, meanwhile):
    seq_bits = bits_of("seq")
    near = list(range(seq_bits - 1, 0, -1))
    state = [x.reshape((1,) * (1 + seq_bits) + x.shape) for x in parts]
    for hop in range(seq_bits + 1):
        if hop == 1:
            *state, meanwhile = together(*state, meanwhile)
        for turn, y in enumerate(state):
            what = (["shard"] + near + [0] if turn % 2 == 0 else near + ["shard", 0])[hop]
            if what == "shard":
                state[turn] = all_blocks(y, "shard", 0)
            else:
                state[turn] = both_halves(y, "seq", what, seq_bits - what)
    return [y.reshape(-1, y.shape[-1]) for y in state], meanwhile


def half_kept(x, axis, bit, dim):
    low = lax.index_in_dim(x, 0, dim)
    high = lax.index_in_dim(x, 1, dim)
    mine = bit_at(axis, bit) == 1
    got = exchange(jnp.where(mine, low, high), axis, 1 << bit)
    kept = jnp.where(mine, high, low)
    return (kept.astype(jnp.float32) + got.astype(jnp.float32)).astype(jnp.bfloat16)


def rep_sums(y):
    total = y.astype(jnp.float32)
    for bit in range(bits_of("rep")):
        y = total.astype(jnp.bfloat16)
        total = y.astype(jnp.float32) + exchange(y, "rep", 1 << bit).astype(jnp.float32)
    return total


def blocks_of(x):
    bits = bits_of("shard") + bits_of("seq")
    return x.reshape((2,) * bits + (x.shape[0] >> bits, x.shape[1]))


def scatter_hop(state, hop):
    seq_bits, shard_bits = bits_of("seq"), bits_of("shard")
    far = [("shard", b) for b in range(shard_bits - 1, -1, -1)]
    near = [("seq", b) for b in range(seq_bits - 1, 0, -1)]
    out = []
    for turn, x in enumerate(state):
        axis, bit = ([("seq", 0)] + (near + far if turn % 2 == 0 else far + near))[hop]
        dim = shard_bits - 1 - bit if axis == "shard" else shard_bits + seq_bits - 1 - bit
        out.append(half_kept(x, axis, bit, dim))
    return out


def sum_everywhere(x):
    for axis in ("seq", "shard", "rep"):
        for bit in range(bits_of(axis)):
            x = x + exchange(x, axis, 1 << bit)
    return x


def together(*values):
    return lax.optimization_barrier(values)


def rms_norm(vectors, gains):
    return (
        vectors * lax.rsqrt(jnp.mean(vectors * vectors, axis=-1, keepdims=True) + EPSILON) * gains
    )


def dot_tn(a, b):
    return lax.dot_general(a, b, (((0,), (0,)), ((), ())), preferred_element_type=jnp.float32)


def wide_row(values):
    row = jnp.pad(values.astype(jnp.float32), (0, SUB - values.shape[0]))
    return jnp.broadcast_to(row[None, :], (8, SUB))


def routed_across(x):
    return lax.all_to_all(x, GROUP, split_axis=0, concat_axis=0, tiled=True)


def prepare_kernel(experts, capacity, parts, len_ref, first_ref, ids_ref, cot_ref, *refs):
    qf_ref, kf_ref, live_ref = refs[:3]
    hot_refs, sent_refs = refs[3 : 3 + len(parts)], refs[3 + len(parts) :]
    ends = [len_ref[0, 0]]
    for d in range(1, DOCS):
        ends.append(ends[-1] + len_ref[0, d])
    first = first_ref[0]
    rows, span = qf_ref.shape[0], kf_ref.shape[0]

    def doc_of(places):
        return sum((places >= end).astype(jnp.int32) for end in ends)

    places = first + lax.broadcasted_iota(jnp.int32, (rows, SUB), 0)
    lane = lax.broadcasted_iota(jnp.int32, (rows, SUB), 1)
    hit = (doc_of(places) == lane) & (lane < DOCS)
    qf_ref[...] = jnp.where(hit, 1.0, 0.0).astype(jnp.bfloat16)
    live_ref[...] = jnp.where(places < ends[-1], 1.0, 0.0).astype(jnp.bfloat16)
    places = first - HALF + lax.broadcasted_iota(jnp.int32, (span, SUB), 0)
    lane = lax.broadcasted_iota(jnp.int32, (span, SUB), 1)
    hit = (doc_of(places) == lane) & (places >= 0) & (places < ends[-1])
    kf_ref[...] = jnp.where((lane < DOCS) & ~hit, MASKED_SCORE, 0.0).astype(jnp.bfloat16)

    live = first + lax.broadcasted_iota(jnp.int32, (1, rows), 1) < ends[-1]
    expert = lax.broadcasted_iota(jnp.int32, (experts, rows), 0)
    chosen = jnp.where((ids_ref[...] == expert) & live, 1.0, 0.0)
    before = lax.broadcasted_iota(jnp.int32, (rows, rows), 0)
    upto = before <= lax.broadcasted_iota(jnp.int32, (rows, rows), 1)
    ranked = dot(chosen.astype(jnp.bfloat16), jnp.where(upto, 1.0, 0.0).astype(jnp.bfloat16))
    slot = chosen * (ranked - 1.0 + capacity * expert.astype(jnp.float32))
    slot = jnp.where(live, jnp.sum(slot, axis=0, keepdims=True), -1.0)
    for (start, stop), hot_ref, sent_ref in zip(parts, hot_refs, sent_refs):
        size = stop - start
        for r in row_chunks(hot_ref.shape[0]):
            shape = (r.stop - r.start, rows)
            place = (r.start + lax.broadcasted_iota(jnp.int32, shape, 0)).astype(jnp.float32)
            owner = jnp.floor((place + 0.5) * (1.0 / size))
            held = owner * capacity + start + (place - owner * size)
            hot = jnp.where(slot == held, 1.0, 0.0).astype(jnp.bfloat16)
            hot_ref[r, :] = hot
            sent_ref[r, :] = dot(hot, cot_ref[...]).astype(jnp.bfloat16)


def prepare(doc_lengths, first_place, expert_ids, cotangent, experts, capacity, parts):
    rows = cotangent.shape[0]
    span = rows + 2 * HALF
    sizes = [experts * (stop - start) for start, stop in parts]
    narrow = lambda n: jax.ShapeDtypeStruct((n, SUB), jnp.bfloat16)
    smem = pl.BlockSpec(memory_space=pltpu.SMEM)
    vmem = pl.BlockSpec(memory_space=pltpu.VMEM)
    out = pl.pallas_call(
        functools.partial(prepare_kernel, experts, capacity, parts),
        in_specs=[smem, smem, vmem, vmem],
        out_specs=[vmem] * (3 + 2 * len(parts)),
        out_shape=[narrow(rows), narrow(span), narrow(rows)]
        + [jax.ShapeDtypeStruct((size, rows), jnp.bfloat16) for size in sizes]
        + [jax.ShapeDtypeStruct((size, D), jnp.bfloat16) for size in sizes],
        compiler_params=pltpu.CompilerParams(vmem_limit_bytes=VMEM_LIMIT),
        cost_estimate=pl.CostEstimate(
            flops=2 * sum(sizes) * rows * D, bytes_accessed=8_000_000, transcendentals=0
        ),
    )(doc_lengths, first_place.reshape(1), expert_ids.reshape(1, rows), cotangent)
    return *out[:3], out[3 : 3 + len(parts)], out[3 + len(parts) :]


def shards(
    tokens,
    doc_lengths,
    expert_ids,
    cotangent,
    gain_attn,
    gain_ffn,
    w_query,
    w_key,
    w_value,
    w_attn_out,
    rel_table,
    w_router,
    w_expert_in,
    w_expert_out,
):
    rows = tokens.shape[0]
    seq_count = lax.axis_size("seq")
    rep_count = lax.axis_size("rep")
    experts = lax.axis_size(GROUP)
    all_devices = lax.axis_size(EVERY)
    capacity = 5 * rows // (4 * experts)
    slots = experts * capacity
    shard_rows = w_query.shape[0]
    table_rows = rel_table.shape[0]
    w_in, w_out = w_expert_in[0], w_expert_out[0]

    def across(values):
        return routed_across(values.reshape(experts, -1, D)).reshape(-1, D)

    def collected(pieces):
        return sum(dot_tn(hot, piece) for hot, piece in zip(hots, pieces))

    def joined(pieces):
        return jnp.concatenate([p.reshape(experts, -1, D) for p in pieces], axis=1).reshape(slots, D)

    def split(values):
        values = values.reshape(experts, capacity, D)
        return [values[:, start:stop].reshape(-1, D) for start, stop in parts]

    few = capacity // 2 // 16 * 16
    parts = [(0, few), (few, capacity)] if few else [(0, capacity)]
    first_place = lax.axis_index("seq") * rows
    q_feat, k_feat, live, hots, cot_sent = prepare(
        doc_lengths, first_place, expert_ids, cotangent, experts, capacity, parts
    )
    is_live = first_place + jnp.arange(rows, dtype=jnp.int32) < jnp.sum(doc_lengths)
    chosen = (expert_ids == jnp.arange(experts, dtype=jnp.int32)[None, :]) & is_live[:, None]
    is_live, chosen_f = is_live.astype(jnp.float32)[:, None], chosen.astype(jnp.float32)
    counts = jnp.sum(chosen_f, axis=0)

    up = [(i, i + 1) for i in range(seq_count - 1)]
    down = [(i + 1, i) for i in range(seq_count - 1)]
    token_span = jnp.concatenate(
        [lax.ppermute(tokens[rows - HALF :], "seq", up), tokens, lax.ppermute(tokens[:HALF], "seq", down)],
        axis=0,
    )
    small = jnp.concatenate(
        [
            w_router,
            gain_attn[:, None],
            gain_ffn[:, None],
            jnp.pad(rel_table, ((0, shard_rows - table_rows), (0, 0))),
            jnp.broadcast_to(counts.astype(jnp.bfloat16)[None, :], (shard_rows, experts)),
        ],
        axis=1,
    )
    small = jnp.pad(small, ((0, 0), (0, SUB - small.shape[1])))
    (w_q, w_k, w_v), cot_sent = gather_rows(
        [jnp.concatenate([w_query, small], axis=1), w_key, w_value], joined(cot_sent)
    )
    w_q, extra = w_q[:, :D], w_q[:, D:]
    router = extra[:, :experts]
    router_wide = jnp.pad(router, ((0, 0), (0, SUB - experts)))
    g_attn = extra[:, experts].astype(jnp.float32)
    g_ffn = extra[:, experts + 1].astype(jnp.float32)
    blocks = extra.reshape(experts, shard_rows, SUB)
    table = blocks[:, :table_rows, experts + 2 : experts + 2 + HEADS]
    table = table.reshape(BUCKETS, HEADS).astype(jnp.float32)
    counts_at = experts + 2 + HEADS
    counts_all = jnp.sum(blocks[:, 0, counts_at : counts_at + experts].astype(jnp.float32), axis=0)
    for bit in range(bits_of("rep")):
        counts_all = counts_all + exchange(counts_all, "rep", 1 << bit)
    live_all = jnp.sum(counts_all)
    shares = counts_all / live_all
    me = lax.axis_index(GROUP)
    pick = wide_row(jnp.arange(experts) == me)
    aux = wide_row((AUX_WEIGHT * experts / live_all) * shares)

    w_attn_out, cot_sent, w_q, w_k, w_v = together(w_attn_out, cot_sent, w_q, w_k, w_v)
    w_proj = lax.all_gather(w_attn_out, GROUP, axis=0, tiled=True)
    cot_rows = across(cot_sent)

    inputs = tokens.astype(jnp.float32)
    normed_span = rms_norm(token_span.astype(jnp.float32), g_attn).astype(jnp.bfloat16)
    normed_one = normed_span[HALF : HALF + rows]
    queries = dot(normed_one, w_q).astype(jnp.bfloat16)
    keys = dot(normed_span, w_k).astype(jnp.bfloat16)
    values = dot(normed_span, w_v).astype(jnp.bfloat16)
    bias_rows = jnp.einsum("rxb,bh->hrx", one_hot(bias_buckets()), table, precision=PRECISE)
    context, expo, inverse = attention_forward(queries, keys, values, q_feat, k_feat, live, bias_rows)
    hidden_state = inputs + dot(context, w_proj)

    ffn_normed, ffn_pull = jax.vjp(rms_norm, hidden_state, g_ffn)
    normed_two = ffn_normed.astype(jnp.bfloat16)
    x_sent = [dot(hot, normed_two).astype(jnp.bfloat16) for hot in hots]
    x_sent[0], cot_rows = together(x_sent[0], cot_rows)
    x_parts = []
    for sent in x_sent:
        if x_parts:
            sent, x_parts[-1] = together(sent, x_parts[-1])
        x_parts.append(across(sent))
    cot_parts = split(cot_rows)
    if rep_count == 2:
        cot_other = exchange(cot_rows, "rep", 1)
        x_other = [exchange(x, "rep", 1) for x in x_parts]
        x_parts[0], x_other[0] = together(x_parts[0], x_other[0])
    done = []
    for x, c in zip(x_parts, cot_parts):
        done.append(expert_pass(x, c, router_wide, pick, aux, w_in, w_out, experts))
    out_parts, back_parts, acts, d_pres, d_row_parts, d_logit_parts = zip(*done)
    blank = [jnp.zeros(shape, jnp.float32) for shape in ((D, WTILE), (WTILE, D))]
    d_expert = weight_pass((x_parts, d_row_parts, acts, d_pres), blank, 0)
    back_all = across(joined(back_parts))
    if rep_count == 2:
        hidden = []
        for x, c in zip(x_other, split(cot_other)):
            hidden += hidden_pass(x, c, router_wide, pick, w_in, w_out, experts)
        back_all, *rest = together(back_all, *d_expert, *hidden)
        d_expert, hidden = rest[:2], rest[2:]
    d_normed_two = collected(split(back_all))
    d_normed_two, *out_parts = together(d_normed_two, *out_parts)
    out_all = across(joined(out_parts))
    d_router = sum(dot_tn(x, d) for x, d in zip(x_parts, d_logit_parts))[:, :experts]

    router_probs = jax.nn.softmax(dot(normed_two, router), axis=-1)
    gating = jnp.sum(router_probs * chosen_f, axis=1)
    hidden_back, d_gain_ffn = ffn_pull(d_normed_two)
    d_hidden = cotangent.astype(jnp.float32) + hidden_back
    d_attn = d_hidden.astype(jnp.bfloat16)
    d_context = dot_nt(d_attn, w_proj).astype(jnp.bfloat16)
    d_attn_out = dot_tn(context, d_attn)
    more = jnp.concatenate([d_router, d_gain_ffn[:, None]], axis=1)
    more = jnp.pad(more, ((0, 0), (0, SUB - more.shape[1])))

    d_q, d_k, d_v, d_bias = attention_backward(
        queries, keys, values, live, expo, inverse, context, d_context, 0, PAIRS
    )
    d_q, d_k, d_v, out_all = together(d_q, d_k, d_v, out_all)
    d_table = jnp.einsum("hrx,rxb->bh", d_bias, one_hot(grad_buckets()), precision=PRECISE)
    d_table = jnp.pad(
        d_table.reshape(experts, table_rows, HEADS), ((0, 0), (0, shard_rows - table_rows), (0, 0))
    ).reshape(D, HEADS)
    more = jnp.concatenate([d_router, d_gain_ffn[:, None], d_table], axis=1)
    more = jnp.pad(more, ((0, 0), (0, SUB - more.shape[1])))
    d_query, d_key, d_value = (
        dot_tn(n, d) for n, d in ((normed_one, d_q), (normed_span, d_k), (normed_span, d_v))
    )
    grads = [
        jnp.concatenate([g.astype(jnp.bfloat16) for g in pair], axis=1)
        for pair in ((d_query, d_attn_out, more), (d_key, d_value))
    ]
    mass = jnp.sum(router_probs * is_live, axis=0)
    mass, *grads = together(mass, *grads)
    mass_all = sum_everywhere(mass)
    grads = [blocks_of(g) for g in grads]
    for hop in range(bits_of("shard") + bits_of("seq")):
        grads = scatter_hop(grads, hop)
        if hop == 0 and rep_count == 2:
            *grads, x_other[0] = together(*grads, x_other[0])
            rows_other = (x_other, hidden[2::3], hidden[0::3], hidden[1::3])
            d_expert = weight_pass(rows_other, d_expert, 1)
        if hop == 1:
            *grads, d_q, d_k, d_v = together(*grads, d_q, d_k, d_v)
        if hop == 2:
            *grads, out_all = together(*grads, out_all)
    d_span = dot_nt(d_k, w_k) + dot_nt(d_v, w_v)
    d_own = d_span[HALF : HALF + rows] + dot_nt(d_q, w_q)
    from_above = lax.ppermute(d_span[:HALF].astype(jnp.bfloat16), "seq", down)
    from_below = lax.ppermute(d_span[HALF + rows :].astype(jnp.bfloat16), "seq", up)
    if rep_count != 2:
        d_expert = [
            lax.psum(g.astype(jnp.bfloat16), "rep").astype(jnp.float32) for g in d_expert
        ]
    left, right = (rep_sums(g.reshape(shard_rows, -1)) for g in grads)
    d_query, d_attn_out, more = left[:, :D], left[:, D : 2 * D], left[:, 2 * D :]
    d_key, d_value = right[:, :D], right[:, D:]
    d_gain_attn = sum(
        jnp.sum(g * w.astype(jnp.float32), axis=1)
        for g, w in ((d_query, w_query), (d_key, w_key), (d_value, w_value))
    ) / gain_attn.astype(jnp.float32)
    balance = experts * jnp.sum(shares * mass_all) / live_all
    importance = experts * mass_all / (rows * all_devices)
    expert_rows = collected(split(out_all))
    mixed = (hidden_state + gating[:, None] * expert_rows).astype(jnp.bfloat16)
    gap = jnp.zeros((rows - HALF, D), jnp.float32)
    d_normed_one = (
        d_own
        + jnp.concatenate([from_below.astype(jnp.float32), gap], axis=0)
        + jnp.concatenate([gap, from_above.astype(jnp.float32)], axis=0)
    )
    _, attn_pull = jax.vjp(lambda v: rms_norm(v, g_attn), inputs)
    d_tokens = d_hidden + attn_pull(d_normed_one)[0]
    return (
        mixed,
        balance,
        importance,
        d_tokens,
        d_gain_attn,
        more[:, experts],
        d_query,
        d_key,
        d_value,
        d_attn_out,
        more[:table_rows, experts + 1 : experts + 1 + HEADS],
        more[:, :experts],
        d_expert[0][None],
        d_expert[1][None],
    )


def solution(mesh):
    split = P(EVERY, None)
    shared = P(GROUP, None)
    gains = P(GROUP)
    stacked = P(GROUP, None, None)
    weights = (shared,) * 6 + (stacked,) * 2
    return jax.shard_map(
        shards,
        mesh=mesh,
        in_specs=(split, P(("rep", "shard"), None), split, split, gains, gains) + weights,
        out_specs=(split, P(), P(), split, gains, gains) + weights,
        check_vma=False,
    )
```

```python
import functools
import math

import jax
import jax.numpy as jnp
import numpy as np
from jax import lax
from jax.experimental import pallas as pl
from jax.experimental.layout import Layout, with_layout_constraint
from jax.experimental.pallas import tpu as pltpu
from jax.sharding import PartitionSpec as P

D = 768
HEADS = 12
HEAD = 64
BUCKETS = 32
MAXDIST = 128
WINDOW = 1024
DOCS = 4
MASKED_SCORE = -1e30
HALF = WINDOW // 2
QB = 256
SUB = 128
KB = QB + WINDOW
PAIRS = HEADS // 2
VMEM_LIMIT = 56 * 1024 * 1024


def thresholds(max_distance, half_count):
    exact_span = half_count // 2
    collected = list(range(1, exact_span + 1))
    for target_level in range(exact_span + 1, half_count):
        candidate = exact_span
        while (
            exact_span
            + int(
                math.log(candidate / exact_span)
                / math.log(max_distance / exact_span)
                * (half_count - exact_span)
            )
            < target_level
        ):
            candidate += 1
        collected.append(candidate)
    return collected


LIMITS = thresholds(MAXDIST, BUCKETS // 2)
assert LIMITS[-1] <= SUB


def bucket_table(distance):
    distance = np.asarray(distance)
    magnitude = np.abs(distance)
    bucket_id = (distance > 0).astype(np.int32) * (BUCKETS // 2)
    for boundary in LIMITS:
        bucket_id = bucket_id + (magnitude >= boundary)
    return bucket_id


def bias_buckets():
    lane = np.arange(2 * SUB)
    rows = []
    for m in (-1, 0, 1):
        rows.append(bucket_table(SUB * m - lane + np.where(lane >= SUB, 2 * SUB, 0)))
    rows.append(np.full(2 * SUB, bucket_table(-WINDOW)))
    rows.append(np.full(2 * SUB, bucket_table(WINDOW)))
    rows += [np.zeros(2 * SUB, np.int32)] * 3
    return np.stack(rows)


def grad_buckets():
    lane = np.arange(SUB)
    rows = [bucket_table(SUB * m - lane) for m in (-1, 0, 1)]
    rows += [bucket_table(SUB * (m + 1) - lane) for m in (-1, 0, 1)]
    rows.append(np.full(SUB, bucket_table(-WINDOW)))
    rows.append(np.full(SUB, bucket_table(WINDOW)))
    return np.stack(rows)


def one_hot(ids):
    return (ids[..., None] == np.arange(BUCKETS)).astype(np.float32)


def dot(a, b):
    return jnp.dot(a, b, preferred_element_type=jnp.float32)


def dot_nt(a, b):
    return lax.dot_general(a, b, (((1,), (1,)), ((), ())), preferred_element_type=jnp.float32)


def head_lanes(shape, axis, h):
    place = lax.broadcasted_iota(jnp.int32, shape, axis)
    return (place < HEAD) if h == 0 else (place >= HEAD)


def fold8(x, op):
    return op(x.reshape(x.shape[0] // 8, 8, x.shape[1]), axis=0)


def block_kind(a, b):
    m = a - b - 4
    return m, "n" if m < -1 else "p" if m > 1 else "v"


def forward_kernel(
    q_ref,
    k_ref,
    v_ref,
    qf_ref,
    kf_ref,
    live_ref,
    w_ref,
    ctx_ref,
    e_ref,
    inv_ref,
    vt,
    bias,
    s_ref,
    peak_ref,
):
    steps = q_ref.shape[0] // QB
    for h in range(2):
        for m in range(3):
            row = jnp.broadcast_to(w_ref[h, m : m + 1, :], (SUB, 2 * SUB))
            bias[h, m] = pltpu.roll(row, 0, 1, stride=1, stride_axis=0)[:, :SUB]
    for s in range(v_ref.shape[0] // QB):
        vt[:, s * QB : (s + 1) * QB] = v_ref[s * QB : (s + 1) * QB, :].T
    row_id = lax.broadcasted_iota(jnp.int32, (SUB, SUB), 0)
    col_id = lax.broadcasted_iota(jnp.int32, (SUB, SUB), 1)

    def stage(score, weigh):
        if score is not None:
            s_now, p_now = s_ref.at[score % 2], peak_ref.at[score % 2]
            rows = pl.ds(pl.multiple_of(score * QB, QB), QB)
            q, qf = q_ref[rows, :], qf_ref[rows, :]
            qx = [
                jnp.concatenate([jnp.where(head_lanes(q.shape, 1, h), q, 0), qf], axis=1)
                for h in range(2)
            ]
            tops = {}
        if weigh is not None:
            s_then, p_then = s_ref.at[weigh % 2], peak_ref.at[weigh % 2]
            totals = {(h, b): jnp.zeros((8, SUB), jnp.float32) for h in range(2) for b in range(2)}
            ct = [jnp.zeros((HEAD, QB), jnp.float32)] * 2
        for c in range(KB // QB):
            if score is not None:
                place = pl.ds(pl.multiple_of(score * QB + c * QB, QB), QB)
                kx = jnp.concatenate([k_ref[place, :], kf_ref[place, :]], axis=1)
                scores = [dot_nt(kx, qx[h]) for h in range(2)]
            if weigh is not None:
                place = pl.ds(pl.multiple_of(weigh * QB + c * QB, QB), QB)
                for h in range(2):
                    chunk = []
                    for a in range(2 * c, 2 * c + 2):
                        line = []
                        for b in range(2):
                            m, kind = block_kind(a, b)
                            if abs(m) > 4:
                                line.append(jnp.zeros((SUB, SUB), jnp.bfloat16))
                                continue
                            row = 3 * h + "nvp".index(kind)
                            cols = slice(b * SUB, (b + 1) * SUB)
                            e = jnp.exp(
                                s_then[h, a * SUB : (a + 1) * SUB, cols] - p_then[row : row + 1, cols]
                            )
                            totals[h, b] = totals[h, b] + fold8(e, jnp.sum)
                            line.append(e.astype(jnp.bfloat16))
                        chunk.append(jnp.concatenate(line, axis=1))
                    chunk = jnp.concatenate(chunk, axis=0)
                    e_ref[0, weigh, h, c * QB : (c + 1) * QB, :] = chunk
                    ct[h] = ct[h] + dot(vt[h * HEAD : (h + 1) * HEAD, place], chunk)
            if score is None:
                continue
            for h in range(2):
                for a in range(2 * c, 2 * c + 2):
                    for b in range(2):
                        m, kind = block_kind(a, b)
                        if abs(m) > 4:
                            continue
                        x = scores[h][
                            (a - 2 * c) * SUB : (a - 2 * c + 1) * SUB, b * SUB : (b + 1) * SUB
                        ]
                        if m == -4:
                            x = jnp.where(row_id >= col_id, x, MASKED_SCORE)
                        if m == 4:
                            x = jnp.where(row_id <= col_id, x, MASKED_SCORE)
                        if kind == "v":
                            x = x + bias[h, m + 1]
                        s_now[h, a * SUB : (a + 1) * SUB, b * SUB : (b + 1) * SUB] = x
                        top = fold8(x, jnp.max)
                        old = tops.get((h, b, kind))
                        tops[h, b, kind] = top if old is None else jnp.maximum(old, top)
        if score is not None:
            for h in range(2):
                neg, pos = w_ref[h, 3:4, :SUB], w_ref[h, 4:5, :SUB]
                for b in range(2):
                    peak = jnp.maximum(
                        jnp.maximum(tops[h, b, "n"] + neg, tops[h, b, "p"] + pos), tops[h, b, "v"]
                    )
                    peak = jnp.max(peak, axis=0, keepdims=True)
                    p_now[3 * h : 3 * h + 3, b * SUB : (b + 1) * SUB] = jnp.concatenate(
                        [peak - neg, peak, peak - pos], axis=0
                    )
        if weigh is not None:
            contexts = []
            for h in range(2):
                total = [jnp.sum(totals[h, b], axis=0, keepdims=True) for b in range(2)]
                inv = 1.0 / jnp.concatenate(total, axis=1)
                inv_ref[0, weigh, h : h + 1, :] = inv
                contexts.append(ct[h] * inv)
            context = jnp.concatenate(contexts, axis=0).T.astype(jnp.bfloat16)
            rows = pl.ds(pl.multiple_of(weigh * QB, QB), QB)
            own = v_ref[pl.ds(pl.multiple_of(weigh * QB + HALF, QB), QB), :]
            ctx_ref[rows, :] = jnp.where(live_ref[rows, :] > 0, context, own)

    stage(0, None)

    def both(t, _):
        stage(t, t - 1)
        return 0

    lax.fori_loop(1, steps, both, 0)
    stage(None, steps - 1)


def backward_kernel(
    q_ref,
    k_ref,
    v_ref,
    live_ref,
    e_ref,
    inv_ref,
    ctx_ref,
    dctx_ref,
    dq_ref,
    dk_ref,
    dv_ref,
    db_ref,
    kt,
    dk_acc,
    dv_acc,
    acc,
    far,
):
    steps = q_ref.shape[0] // QB
    for s in range(k_ref.shape[0] // QB):
        kt[:, s * QB : (s + 1) * QB] = k_ref[s * QB : (s + 1) * QB, :].T
    dk_acc[...] = jnp.zeros_like(dk_acc)
    dv_acc[...] = jnp.zeros_like(dv_acc)
    acc[...] = jnp.zeros_like(acc)
    far[...] = jnp.zeros_like(far)

    def block(i, _):
        rows = pl.ds(pl.multiple_of(i * QB, QB), QB)
        q = q_ref[rows, :]
        dctx = dctx_ref[rows, :].astype(jnp.float32)
        kept = jnp.where(live_ref[rows, :] > 0, dctx, 0.0)
        prod = (kept * ctx_ref[rows, :].astype(jnp.float32)).T
        kept_t = kept.T
        qs, dts, deltas = [], [], []
        for h in range(2):
            inv = inv_ref[0, i, h : h + 1, :]
            qs.append(jnp.where(head_lanes(q.shape, 1, h), q, 0))
            dts.append(
                jnp.where(head_lanes(kept_t.shape, 0, h), kept_t * inv, 0.0).astype(jnp.bfloat16)
            )
            deltas.append(jnp.sum(prod[h * HEAD : (h + 1) * HEAD], axis=0, keepdims=True) * inv)
        q_both = jnp.concatenate(qs, axis=0)
        dt_both = jnp.concatenate(dts, axis=1)
        fars = [[jnp.zeros((8, SUB), jnp.float32)] * 2 for _ in range(2)]
        dqt = [jnp.zeros((HEAD, QB), jnp.float32)] * 2

        def places(c):
            return pl.ds(pl.multiple_of(i * QB + c * QB, QB), QB)

        def products(c):
            vc = v_ref[places(c), :]
            return [dot(vc, dts[h]) for h in range(2)]

        ahead = products(0)
        for c in range(KB // QB):
            place = places(c)
            dps = ahead
            if c + 1 < KB // QB:
                ahead = products(c + 1)
            grads, weights = [], []
            for h in range(2):
                e = e_ref[0, i, h, c * QB : (c + 1) * QB, :]
                ds = e.astype(jnp.float32) * (dps[h] - deltas[h])
                for a in range(2 * c, 2 * c + 2):
                    for b in range(2):
                        m, kind = block_kind(a, b)
                        x = ds[(a - 2 * c) * SUB : (a - 2 * c + 1) * SUB, b * SUB : (b + 1) * SUB]
                        if abs(m) > 4:
                            continue
                        if kind == "v":
                            acc[h, m + 1] += x
                        else:
                            side = "np".index(kind)
                            fars[h][side] = fars[h][side] + fold8(x, jnp.sum)
                ds = ds.astype(jnp.bfloat16)
                dqt[h] = dqt[h] + dot(kt[h * HEAD : (h + 1) * HEAD, place], ds)
                grads.append(ds)
                weights.append(e)
            dk_acc[place, :] += dot(jnp.concatenate(grads, axis=1), q_both)
            dv_acc[place, :] += dot_nt(jnp.concatenate(weights, axis=1), dt_both)
        dq_ref[rows, :] = jnp.concatenate(dqt, axis=0).T.astype(jnp.bfloat16)
        own = pl.ds(pl.multiple_of(i * QB + HALF, QB), QB)
        dv_acc[own, :] += dctx - kept
        for h in range(2):
            for side in range(2):
                far[h, side] += fars[h][side]
        return 0

    lax.fori_loop(0, steps, block, 0)
    dk_ref[...] = dk_acc[...].astype(jnp.bfloat16)
    dv_ref[...] = dv_acc[...].astype(jnp.bfloat16)
    row_id = lax.broadcasted_iota(jnp.int32, (SUB, SUB), 0)
    col_id = lax.broadcasted_iota(jnp.int32, (SUB, SUB), 1)
    sublane = lax.broadcasted_iota(jnp.int32, (8, SUB), 0)
    for h in range(2):
        sums = []
        for upper in (True, False):
            for m in range(3):
                x = jnp.where((col_id >= row_id) == upper, acc[h, m], 0.0)
                y = x[:8]
                for g in range(1, SUB // 8):
                    y = y + pltpu.roll(x[8 * g : 8 * g + 8], SUB - 8 * g, 1)
                for bit in range(3):
                    y = jnp.where(
                        (sublane >> bit) % 2 == 1, pltpu.roll(y, SUB - (1 << bit), 1), y
                    )
                sums.append(jnp.sum(y, axis=0, keepdims=True))
        for side in range(2):
            sums.append(jnp.sum(far[h, side], axis=0, keepdims=True))
        db_ref[h] = jnp.concatenate(sums, axis=0)


def spec(shape, index):
    return pl.BlockSpec(shape, index)


def attention_forward(queries, keys, values, q_feat, k_feat, live, bias_rows):
    rows, span = queries.shape[0], keys.shape[0]
    steps = rows // QB
    return pl.pallas_call(
        forward_kernel,
        grid=(PAIRS,),
        in_specs=[
            spec((rows, SUB), lambda p: (0, p)),
            spec((span, SUB), lambda p: (0, p)),
            spec((span, SUB), lambda p: (0, p)),
            spec((rows, SUB), lambda p: (0, 0)),
            spec((span, SUB), lambda p: (0, 0)),
            spec((rows, SUB), lambda p: (0, 0)),
            spec((2, 8, 2 * SUB), lambda p: (p, 0, 0)),
        ],
        out_specs=[
            spec((rows, SUB), lambda p: (0, p)),
            spec((1, steps, 2, KB, QB), lambda p: (p, 0, 0, 0, 0)),
            spec((1, steps, 8, QB), lambda p: (p, 0, 0, 0)),
        ],
        out_shape=[
            jax.ShapeDtypeStruct((rows, D), jnp.bfloat16),
            jax.ShapeDtypeStruct((PAIRS, steps, 2, KB, QB), jnp.bfloat16),
            jax.ShapeDtypeStruct((PAIRS, steps, 8, QB), jnp.float32),
        ],
        scratch_shapes=[
            pltpu.VMEM((SUB, span), jnp.bfloat16),
            pltpu.VMEM((2, 3, SUB, SUB), jnp.float32),
            pltpu.VMEM((2, 2, KB, QB), jnp.float32),
            pltpu.VMEM((2, 8, QB), jnp.float32),
        ],
        compiler_params=pltpu.CompilerParams(
            dimension_semantics=("arbitrary",), vmem_limit_bytes=VMEM_LIMIT
        ),
        cost_estimate=pl.CostEstimate(
            flops=4 * rows * KB * D * 4, bytes_accessed=45_000_000, transcendentals=rows * KB * HEADS
        ),
    )(queries, keys, values, q_feat, k_feat, live, bias_rows)


def attention_backward(
    queries, keys, values, live, expo, inverse, context, d_context, first, pairs
):
    rows, span = queries.shape[0], keys.shape[0]
    steps = rows // QB
    return pl.pallas_call(
        backward_kernel,
        grid=(pairs,),
        in_specs=[
            spec((rows, SUB), lambda p: (0, p + first)),
            spec((span, SUB), lambda p: (0, p + first)),
            spec((span, SUB), lambda p: (0, p + first)),
            spec((rows, SUB), lambda p: (0, 0)),
            spec((1, steps, 2, KB, QB), lambda p: (p + first, 0, 0, 0, 0)),
            spec((1, steps, 8, QB), lambda p: (p + first, 0, 0, 0)),
            spec((rows, SUB), lambda p: (0, p + first)),
            spec((rows, SUB), lambda p: (0, p + first)),
        ],
        out_specs=[
            spec((rows, SUB), lambda p: (0, p)),
            spec((span, SUB), lambda p: (0, p)),
            spec((span, SUB), lambda p: (0, p)),
            spec((2, 8, SUB), lambda p: (p, 0, 0)),
        ],
        out_shape=[
            jax.ShapeDtypeStruct((rows, pairs * SUB), jnp.bfloat16),
            jax.ShapeDtypeStruct((span, pairs * SUB), jnp.bfloat16),
            jax.ShapeDtypeStruct((span, pairs * SUB), jnp.bfloat16),
            jax.ShapeDtypeStruct((2 * pairs, 8, SUB), jnp.float32),
        ],
        scratch_shapes=[
            pltpu.VMEM((SUB, span), jnp.bfloat16),
            pltpu.VMEM((span, SUB), jnp.float32),
            pltpu.VMEM((span, SUB), jnp.float32),
            pltpu.VMEM((2, 3, SUB, SUB), jnp.float32),
            pltpu.VMEM((2, 2, 8, SUB), jnp.float32),
        ],
        compiler_params=pltpu.CompilerParams(
            dimension_semantics=("arbitrary",), vmem_limit_bytes=VMEM_LIMIT
        ),
        cost_estimate=pl.CostEstimate(
            flops=8 * rows * KB * pairs * SUB * 4, bytes_accessed=9_000_000 * pairs, transcendentals=0
        ),
    )(queries, keys, values, live, expo, inverse, context, d_context)


FF = 3072
TILE = 768
CHUNK = 768
WTILE = 512
WCHUNK = 256


def gelu_parts(v):
    scale = 0.7978845608
    square = v * v
    t = jnp.tanh(scale * v * (1.0 + 0.044715 * square))
    half = 0.5 * (1.0 + t)
    slope = half + 0.5 * v * (1.0 - t * t) * (scale + (3 * 0.044715 * scale) * square)
    return half * v, slope


def routing(x, router, pick, experts):
    logits = dot(x, router)
    lane = lax.broadcasted_iota(jnp.int32, logits.shape, 1)
    logits = jnp.where(lane < experts, logits, MASKED_SCORE)
    expo = jnp.exp(logits - jnp.max(logits, axis=1, keepdims=True))
    probs = expo / jnp.sum(expo, axis=1, keepdims=True)
    return probs, jnp.sum(probs * pick, axis=1, keepdims=True)


def hidden_pair(x, d_rows, w_in, w_out):
    inner, slope = gelu_parts(dot(x, w_in))
    d_pre = dot_nt(d_rows, w_out) * slope
    return inner.astype(jnp.bfloat16), d_pre.astype(jnp.bfloat16)


def row_chunks(rows, size=QB):
    return [slice(s, min(s + size, rows)) for s in range(0, rows, size)]


def expert_kernel(
    experts,
    x_ref,
    c_ref,
    router_ref,
    pick_ref,
    aux_ref,
    win_ref,
    wout_ref,
    rows_ref,
    back_ref,
    act_ref,
    dpre_ref,
    drows_ref,
    dlog_ref,
    probs,
    rows_acc,
    back_acc,
):
    step = pl.program_id(0)
    pick = pick_ref[0:1, :]

    @pl.when(step == 0)
    def _():
        for r in row_chunks(x_ref.shape[0]):
            p, gate = routing(x_ref[r, :], router_ref[...], pick, experts)
            probs[r, :] = p
            drows_ref[r, :] = (gate * c_ref[r, :].astype(jnp.float32)).astype(jnp.bfloat16)
        rows_acc[...] = jnp.zeros_like(rows_acc)
        back_acc[...] = jnp.zeros_like(back_acc)

    w_in, w_out = win_ref[...], wout_ref[...]
    for r in row_chunks(x_ref.shape[0], CHUNK):
        act, dpre = hidden_pair(x_ref[r, :], drows_ref[r, :], w_in, w_out)
        act_ref[r, :] = act
        dpre_ref[r, :] = dpre
        rows_acc[r, :] += dot(act, w_out)
        back_acc[r, :] += dot_nt(dpre, w_in)

    @pl.when(step == pl.num_programs(0) - 1)
    def _():
        for r in row_chunks(x_ref.shape[0]):
            rows = rows_acc[r, :].astype(jnp.bfloat16)
            rows_ref[r, :] = rows
            d_gate = jnp.sum(
                c_ref[r, :].astype(jnp.float32) * rows.astype(jnp.float32), axis=1, keepdims=True
            )
            p = probs[r, :]
            d_probs = pick * d_gate + aux_ref[0:1, :]
            d_log = p * (d_probs - jnp.sum(d_probs * p, axis=1, keepdims=True))
            d_log = d_log.astype(jnp.bfloat16)
            dlog_ref[r, :] = d_log
            back = back_acc[r, :].astype(jnp.bfloat16).astype(jnp.float32)
            back_ref[r, :] = (back + dot_nt(d_log, router_ref[...])).astype(jnp.bfloat16)


def whole(shape):
    return pl.BlockSpec(shape, lambda t: (0,) * len(shape))


def expert_pass(x, cot, router, pick, aux, w_in, w_out, experts):
    rows = x.shape[0]
    wide = jax.ShapeDtypeStruct((rows, FF), jnp.bfloat16)
    narrow = jax.ShapeDtypeStruct((rows, D), jnp.bfloat16)
    return pl.pallas_call(
        functools.partial(expert_kernel, experts),
        grid=(FF // TILE,),
        in_specs=[
            whole((rows, D)),
            whole((rows, D)),
            whole((D, SUB)),
            whole((8, SUB)),
            whole((8, SUB)),
            pl.BlockSpec((D, TILE), lambda t: (0, t)),
            pl.BlockSpec((TILE, D), lambda t: (t, 0)),
        ],
        out_specs=[
            whole((rows, D)),
            whole((rows, D)),
            pl.BlockSpec((rows, TILE), lambda t: (0, t)),
            pl.BlockSpec((rows, TILE), lambda t: (0, t)),
            whole((rows, D)),
            whole((rows, SUB)),
        ],
        out_shape=[narrow, narrow, wide, wide, narrow, jax.ShapeDtypeStruct((rows, SUB), jnp.bfloat16)],
        scratch_shapes=[
            pltpu.VMEM((rows, SUB), jnp.float32),
            pltpu.VMEM((rows, D), jnp.float32),
            pltpu.VMEM((rows, D), jnp.float32),
        ],
        compiler_params=pltpu.CompilerParams(
            dimension_semantics=("arbitrary",), vmem_limit_bytes=VMEM_LIMIT
        ),
        cost_estimate=pl.CostEstimate(
            flops=8 * rows * D * FF, bytes_accessed=30_000_000, transcendentals=rows * FF
        ),
    )(x, cot, router, pick, aux, w_in, w_out)


def transposed(target, source, place):
    for r in row_chunks(source.shape[0]):
        at = pl.multiple_of(place + r.start, QB)
        target[:, pl.ds(at, QB)] = source[r, :].T


def hidden_kernel(experts, x_ref, c_ref, router_ref, pick_ref, win_ref, wout_ref, act_ref, dpre_ref, drows_ref):
    @pl.when(pl.program_id(0) == 0)
    def _():
        for r in row_chunks(x_ref.shape[0]):
            _, gate = routing(x_ref[r, :], router_ref[...], pick_ref[0:1, :], experts)
            drows_ref[r, :] = (gate * c_ref[r, :].astype(jnp.float32)).astype(jnp.bfloat16)

    act, dpre = hidden_pair(x_ref[...], drows_ref[...], win_ref[...], wout_ref[...])
    act_ref[...] = act
    dpre_ref[...] = dpre


def hidden_pass(x, cot, router, pick, w_in, w_out, experts):
    rows = x.shape[0]
    wide = jax.ShapeDtypeStruct((rows, FF), jnp.bfloat16)
    wide_spec = pl.BlockSpec((rows, TILE), lambda t: (0, t))
    return pl.pallas_call(
        functools.partial(hidden_kernel, experts),
        grid=(FF // TILE,),
        in_specs=[
            whole((rows, D)),
            whole((rows, D)),
            whole((D, SUB)),
            whole((8, SUB)),
            pl.BlockSpec((D, TILE), lambda t: (0, t)),
            pl.BlockSpec((TILE, D), lambda t: (t, 0)),
        ],
        out_specs=[wide_spec, wide_spec, whole((rows, D))],
        out_shape=[wide, wide, jax.ShapeDtypeStruct((rows, D), jnp.bfloat16)],
        compiler_params=pltpu.CompilerParams(
            dimension_semantics=("arbitrary",), vmem_limit_bytes=VMEM_LIMIT
        ),
        cost_estimate=pl.CostEstimate(
            flops=4 * rows * D * FF, bytes_accessed=30_000_000, transcendentals=rows * FF
        ),
    )(x, cot, router, pick, w_in, w_out)


def weight_kernel(parts, more_ref, *refs):
    x_refs, drows_refs, act_refs, dpre_refs = (refs[k * parts : (k + 1) * parts] for k in range(4))
    din_old, dout_old, din_ref, dout_ref, xt, d_rows, act_t, dpres = refs[4 * parts :]
    sizes = [x.shape[0] for x in x_refs]
    starts = [sum(sizes[:k]) for k in range(parts)]

    @pl.when(pl.program_id(0) == 0)
    def _():
        for k in range(parts):
            transposed(xt, x_refs[k], starts[k])
            d_rows[starts[k] : starts[k] + sizes[k], :] = drows_refs[k][...]

    for k in range(parts):
        transposed(act_t, act_refs[k], starts[k])
        dpres[starts[k] : starts[k] + sizes[k], :] = dpre_refs[k][...]
    din_ref[...] = dot(xt[...], dpres[...])
    dout_ref[...] = dot(act_t[...], d_rows[...])

    @pl.when(more_ref[0] > 0)
    def _():
        din_ref[...] = din_ref[...] + din_old[...]
        dout_ref[...] = dout_ref[...] + dout_old[...]


def weight_pass(rows_of, old, more):
    sizes = [x.shape[0] for x in rows_of[0]]
    total = sum(sizes)
    narrow = [pl.BlockSpec((rows, D), lambda t, m: (0, 0)) for rows in sizes]
    wide = [pl.BlockSpec((rows, WTILE), lambda t, m: (0, t)) for rows in sizes]
    old_specs = [
        pl.BlockSpec((D, WTILE), lambda t, m: (0, t * m[0])),
        pl.BlockSpec((WTILE, D), lambda t, m: (t * m[0], 0)),
    ]
    new_specs = [
        pl.BlockSpec((D, WTILE), lambda t, m: (0, t)),
        pl.BlockSpec((WTILE, D), lambda t, m: (t, 0)),
    ]
    return pl.pallas_call(
        functools.partial(weight_kernel, len(sizes)),
        grid_spec=pltpu.PrefetchScalarGridSpec(
            num_scalar_prefetch=1,
            grid=(FF // WTILE,),
            in_specs=narrow * 2 + wide * 2 + old_specs,
            out_specs=new_specs,
            scratch_shapes=[
                pltpu.VMEM((D, total), jnp.bfloat16),
                pltpu.VMEM((total, D), jnp.bfloat16),
                pltpu.VMEM((WTILE, total), jnp.bfloat16),
                pltpu.VMEM((total, WTILE), jnp.bfloat16),
            ],
        ),
        out_shape=[
            jax.ShapeDtypeStruct((D, FF), jnp.float32),
            jax.ShapeDtypeStruct((FF, D), jnp.float32),
        ],
        compiler_params=pltpu.CompilerParams(
            dimension_semantics=("arbitrary",), vmem_limit_bytes=VMEM_LIMIT
        ),
        cost_estimate=pl.CostEstimate(
            flops=4 * total * D * FF, bytes_accessed=50_000_000, transcendentals=0
        ),
    )(jnp.full((1,), more, jnp.int32), *[array for group in rows_of for array in group], *old)


EPSILON = 1e-06
AUX_WEIGHT = 0.01
PRECISE = lax.Precision.HIGHEST
GROUP = ("shard", "seq")
EVERY = ("rep", "shard", "seq")


def exchange(x, axis, hop):
    count = lax.axis_size(axis)
    return lax.ppermute(x, axis, [(i, i ^ hop) for i in range(count)])


def bits_of(axis):
    return lax.axis_size(axis).bit_length() - 1


def bit_at(axis, bit):
    return (lax.axis_index(axis) >> bit) & 1


def both_halves(x, axis, bit, dim):
    other = exchange(x, axis, 1 << bit)
    size = x.shape[dim]
    rec = jnp.concatenate([other, x, other], axis=dim)
    return lax.dynamic_slice_in_dim(rec, (1 - bit_at(axis, bit)) * size, 2 * size, axis=dim)


def all_blocks(x, axis, dim):
    count = lax.axis_size(axis)
    size = x.shape[dim]
    turned = [
        lax.ppermute(x, axis, [(i, (i + k) % count) for i in range(count)])
        for k in range(count - 1, 0, -1)
    ]
    rec = jnp.concatenate(turned + [x] + turned, axis=dim)
    start = (count - 1 - lax.axis_index(axis)) * size
    return lax.dynamic_slice_in_dim(rec, start, count * size, axis=dim)


def gather_rows(parts, meanwhile):
    seq_bits = bits_of("seq")
    near = list(range(seq_bits - 1, 0, -1))
    state = [x.reshape((1,) * (1 + seq_bits) + x.shape) for x in parts]
    for hop in range(seq_bits + 1):
        if hop > 0:
            values = together(*state, *meanwhile)
            state, meanwhile = list(values[: len(parts)]), values[len(parts) :]
        for turn, y in enumerate(state):
            what = (["shard"] + near + [0] if turn % 2 == 0 else near + ["shard", 0])[hop]
            if what == "shard":
                state[turn] = all_blocks(y, "shard", 0)
            else:
                state[turn] = both_halves(y, "seq", what, seq_bits - what)
    return [y.reshape(-1, y.shape[-1]) for y in state], meanwhile


def half_kept(x, axis, bit, outer):
    low, high = (x.reshape(outer, 2, -1, x.shape[1])[:, k] for k in range(2))
    mine = bit_at(axis, bit) == 1
    got = exchange(jnp.where(mine, low, high), axis, 1 << bit)
    kept = jnp.where(mine, high, low)
    total = (kept.astype(jnp.float32) + got.astype(jnp.float32)).astype(jnp.bfloat16)
    return total.reshape(-1, x.shape[1])


def rep_sums(y):
    total = y.astype(jnp.float32)
    for bit in range(bits_of("rep")):
        y = total.astype(jnp.bfloat16)
        total = y.astype(jnp.float32) + exchange(y, "rep", 1 << bit).astype(jnp.float32)
    return total


def scatter_order(turn):
    far = [("shard", b) for b in range(bits_of("shard") - 1, -1, -1)]
    near = [("seq", b) for b in range(bits_of("seq") - 1, 0, -1)]
    return [("seq", 0)] + (near + far if turn % 2 == 0 else far + near)


def scatter_hop(state, hop):
    places = [("shard", b) for b in range(bits_of("shard") - 1, -1, -1)]
    places += [("seq", b) for b in range(bits_of("seq") - 1, -1, -1)]
    out = []
    for turn, x in enumerate(state):
        order = scatter_order(turn)
        left = [p for p in places if p not in order[:hop]]
        axis, bit = order[hop]
        out.append(half_kept(x, axis, bit, 1 << left.index((axis, bit))))
    return out


def together(*values):
    return lax.optimization_barrier(values)


def in_rows(x):
    return with_layout_constraint(x, Layout(major_to_minor=(0, 1)))


def rms_norm(vectors, gains):
    return (
        vectors * lax.rsqrt(jnp.mean(vectors * vectors, axis=-1, keepdims=True) + EPSILON) * gains
    )


def dot_tn(a, b):
    return lax.dot_general(a, b, (((0,), (0,)), ((), ())), preferred_element_type=jnp.float32)


def wide_row(values):
    row = jnp.pad(values.astype(jnp.float32), (0, SUB - values.shape[0]))
    return jnp.broadcast_to(row[None, :], (8, SUB))


def routed_across(x):
    return lax.all_to_all(x, GROUP, split_axis=0, concat_axis=0, tiled=True)


def prepare_kernel(experts, capacity, parts, len_ref, first_ref, ids_ref, cot_ref, *refs):
    qf_ref, kf_ref, live_ref = refs[:3]
    hot_refs, sent_refs = refs[3 : 3 + len(parts)], refs[3 + len(parts) :]
    ends = [len_ref[0, 0]]
    for d in range(1, DOCS):
        ends.append(ends[-1] + len_ref[0, d])
    first = first_ref[0]
    rows, span = qf_ref.shape[0], kf_ref.shape[0]

    def doc_of(places):
        return sum((places >= end).astype(jnp.int32) for end in ends)

    places = first + lax.broadcasted_iota(jnp.int32, (rows, SUB), 0)
    lane = lax.broadcasted_iota(jnp.int32, (rows, SUB), 1)
    hit = (doc_of(places) == lane) & (lane < DOCS)
    qf_ref[...] = jnp.where(hit, 1.0, 0.0).astype(jnp.bfloat16)
    live_ref[...] = jnp.where(places < ends[-1], 1.0, 0.0).astype(jnp.bfloat16)
    places = first - HALF + lax.broadcasted_iota(jnp.int32, (span, SUB), 0)
    lane = lax.broadcasted_iota(jnp.int32, (span, SUB), 1)
    hit = (doc_of(places) == lane) & (places >= 0) & (places < ends[-1])
    kf_ref[...] = jnp.where((lane < DOCS) & ~hit, MASKED_SCORE, 0.0).astype(jnp.bfloat16)

    live = first + lax.broadcasted_iota(jnp.int32, (1, rows), 1) < ends[-1]
    expert = lax.broadcasted_iota(jnp.int32, (experts, rows), 0)
    chosen = jnp.where((ids_ref[...] == expert) & live, 1.0, 0.0)
    before = lax.broadcasted_iota(jnp.int32, (rows, rows), 0)
    upto = before <= lax.broadcasted_iota(jnp.int32, (rows, rows), 1)
    ranked = dot(chosen.astype(jnp.bfloat16), jnp.where(upto, 1.0, 0.0).astype(jnp.bfloat16))
    slot = chosen * (ranked - 1.0 + capacity * expert.astype(jnp.float32))
    slot = jnp.where(live, jnp.sum(slot, axis=0, keepdims=True), -1.0)
    for (start, stop), hot_ref, sent_ref in zip(parts, hot_refs, sent_refs):
        size = stop - start
        for r in row_chunks(hot_ref.shape[0]):
            shape = (r.stop - r.start, rows)
            place = (r.start + lax.broadcasted_iota(jnp.int32, shape, 0)).astype(jnp.float32)
            owner = jnp.floor((place + 0.5) * (1.0 / size))
            held = owner * capacity + start + (place - owner * size)
            hot = jnp.where(slot == held, 1.0, 0.0).astype(jnp.bfloat16)
            hot_ref[r, :] = hot
            sent_ref[r, :] = dot(hot, cot_ref[...]).astype(jnp.bfloat16)


def prepare(doc_lengths, first_place, expert_ids, cotangent, experts, capacity, parts):
    rows = cotangent.shape[0]
    span = rows + 2 * HALF
    sizes = [experts * (stop - start) for start, stop in parts]
    narrow = lambda n: jax.ShapeDtypeStruct((n, SUB), jnp.bfloat16)
    smem = pl.BlockSpec(memory_space=pltpu.SMEM)
    vmem = pl.BlockSpec(memory_space=pltpu.VMEM)
    out = pl.pallas_call(
        functools.partial(prepare_kernel, experts, capacity, parts),
        in_specs=[smem, smem, vmem, vmem],
        out_specs=[vmem] * (3 + 2 * len(parts)),
        out_shape=[narrow(rows), narrow(span), narrow(rows)]
        + [jax.ShapeDtypeStruct((size, rows), jnp.bfloat16) for size in sizes]
        + [jax.ShapeDtypeStruct((size, D), jnp.bfloat16) for size in sizes],
        compiler_params=pltpu.CompilerParams(vmem_limit_bytes=VMEM_LIMIT),
        cost_estimate=pl.CostEstimate(
            flops=2 * sum(sizes) * rows * D, bytes_accessed=8_000_000, transcendentals=0
        ),
    )(doc_lengths, first_place.reshape(1), expert_ids.reshape(1, rows), cotangent)
    return *out[:3], out[3 : 3 + len(parts)], out[3 + len(parts) :]


def shards(
    tokens,
    doc_lengths,
    expert_ids,
    cotangent,
    gain_attn,
    gain_ffn,
    w_query,
    w_key,
    w_value,
    w_attn_out,
    rel_table,
    w_router,
    w_expert_in,
    w_expert_out,
):
    rows = tokens.shape[0]
    seq_count = lax.axis_size("seq")
    rep_count = lax.axis_size("rep")
    experts = lax.axis_size(GROUP)
    all_devices = lax.axis_size(EVERY)
    capacity = 5 * rows // (4 * experts)
    slots = experts * capacity
    shard_rows = w_query.shape[0]
    table_rows = rel_table.shape[0]
    w_in, w_out = w_expert_in[0], w_expert_out[0]

    def across(values):
        return routed_across(values.reshape(experts, -1, D)).reshape(-1, D)

    def collected(pieces):
        return sum(dot_tn(hot, piece) for hot, piece in zip(hots, pieces))

    def joined(pieces):
        return jnp.concatenate([p.reshape(experts, -1, D) for p in pieces], axis=1).reshape(slots, D)

    def split(values):
        values = values.reshape(experts, capacity, D)
        return [values[:, start:stop].reshape(-1, D) for start, stop in parts]

    few = capacity // 2 // 16 * 16
    parts = [(0, few), (few, capacity)] if few else [(0, capacity)]
    first_place = lax.axis_index("seq") * rows
    q_feat, k_feat, live, hots, cot_sent = prepare(
        doc_lengths, first_place, expert_ids, cotangent, experts, capacity, parts
    )
    is_live = first_place + jnp.arange(rows, dtype=jnp.int32) < jnp.sum(doc_lengths)
    chosen = (expert_ids == jnp.arange(experts, dtype=jnp.int32)[None, :]) & is_live[:, None]
    is_live, chosen_f = is_live.astype(jnp.float32)[:, None], chosen.astype(jnp.float32)
    counts = jnp.sum(chosen_f, axis=0)

    up = [(i, i + 1) for i in range(seq_count - 1)]
    down = [(i + 1, i) for i in range(seq_count - 1)]
    token_span = jnp.concatenate(
        [lax.ppermute(tokens[rows - HALF :], "seq", up), tokens, lax.ppermute(tokens[:HALF], "seq", down)],
        axis=0,
    )
    small = jnp.concatenate(
        [
            w_router,
            gain_attn[:, None],
            gain_ffn[:, None],
            jnp.pad(rel_table, ((0, shard_rows - table_rows), (0, 0))),
            jnp.broadcast_to(counts.astype(jnp.bfloat16)[None, :], (shard_rows, experts)),
        ],
        axis=1,
    )
    small = jnp.pad(small, ((0, 0), (0, SUB - small.shape[1])))
    (w_q, w_k, w_v), (cot_sent, w_attn_out) = gather_rows(
        [jnp.concatenate([w_query, small], axis=1), w_key, w_value], (joined(cot_sent), w_attn_out)
    )
    w_q, extra = w_q[:, :D], w_q[:, D:]
    router = extra[:, :experts]
    router_wide = jnp.pad(router, ((0, 0), (0, SUB - experts)))
    g_attn = extra[:, experts].astype(jnp.float32)
    g_ffn = extra[:, experts + 1].astype(jnp.float32)
    blocks = extra.reshape(experts, shard_rows, SUB)
    table = blocks[:, :table_rows, experts + 2 : experts + 2 + HEADS]
    table = table.reshape(BUCKETS, HEADS).astype(jnp.float32)
    counts_at = experts + 2 + HEADS
    counts_all = jnp.sum(blocks[:, 0, counts_at : counts_at + experts].astype(jnp.float32), axis=0)
    for bit in range(bits_of("rep")):
        counts_all = counts_all + exchange(counts_all, "rep", 1 << bit)
    live_all = jnp.sum(counts_all)
    shares = counts_all / live_all
    me = lax.axis_index(GROUP)
    pick = wide_row(jnp.arange(experts) == me)
    aux = wide_row((AUX_WEIGHT * experts / live_all) * shares)

    w_proj = lax.all_gather(w_attn_out, GROUP, axis=0, tiled=True)
    cot_rows = across(cot_sent)

    inputs = tokens.astype(jnp.float32)
    normed_span = rms_norm(token_span.astype(jnp.float32), g_attn).astype(jnp.bfloat16)
    normed_one = normed_span[HALF : HALF + rows]
    queries = dot(normed_one, w_q).astype(jnp.bfloat16)
    keys = dot(normed_span, w_k).astype(jnp.bfloat16)
    values = dot(normed_span, w_v).astype(jnp.bfloat16)
    bias_rows = jnp.einsum("rxb,bh->hrx", one_hot(bias_buckets()), table, precision=PRECISE)
    context, expo, inverse = attention_forward(queries, keys, values, q_feat, k_feat, live, bias_rows)
    hidden_state = inputs + dot(context, w_proj)

    ffn_normed, ffn_pull = jax.vjp(rms_norm, hidden_state, g_ffn)
    normed_two = ffn_normed.astype(jnp.bfloat16)
    x_sent = [dot(hot, normed_two).astype(jnp.bfloat16) for hot in hots]
    x_sent[0], cot_rows = together(x_sent[0], cot_rows)
    x_parts = []
    for sent in x_sent:
        if x_parts:
            sent, x_parts[-1] = together(sent, x_parts[-1])
        x_parts.append(across(sent))
    cot_parts = split(cot_rows)
    if rep_count == 2:
        cot_other = exchange(cot_rows, "rep", 1)
        x_other = [exchange(x, "rep", 1) for x in x_parts]
    done = []
    for x, c in zip(x_parts, cot_parts):
        if done:
            x, done[-1][1] = together(x, done[-1][1])
        done.append(list(expert_pass(x, c, router_wide, pick, aux, w_in, w_out, experts)))
    out_parts, back_parts, acts, d_pres, d_row_parts, d_logit_parts = zip(*done)
    blank = [jnp.zeros(shape, jnp.float32) for shape in ((D, WTILE), (WTILE, D))]
    d_expert = weight_pass((x_parts, d_row_parts, acts, d_pres), blank, 0)
    back = [across(p) for p in back_parts]
    if rep_count == 2:
        hidden = []
        for x, c in zip(x_other, split(cot_other)):
            hidden += hidden_pass(x, c, router_wide, pick, w_in, w_out, experts)
        back[-1], *rest = together(back[-1], *d_expert, *hidden)
        d_expert, hidden = rest[:2], rest[2:]
    d_normed_two = collected(back)
    d_normed_two, *out_parts = together(d_normed_two, *out_parts)
    out_all = across(joined(out_parts))
    d_router = sum(dot_tn(x, d) for x, d in zip(x_parts, d_logit_parts))[:, :experts]

    router_probs = jax.nn.softmax(dot(normed_two, router), axis=-1)
    gating = jnp.sum(router_probs * chosen_f, axis=1)
    hidden_back, d_gain_ffn = ffn_pull(d_normed_two)
    d_hidden = cotangent.astype(jnp.float32) + hidden_back
    d_attn = d_hidden.astype(jnp.bfloat16)
    d_context = dot_nt(d_attn, w_proj).astype(jnp.bfloat16)
    d_attn_out = dot_tn(context, d_attn)
    more = jnp.concatenate([d_router, d_gain_ffn[:, None]], axis=1)
    more = jnp.pad(more, ((0, 0), (0, SUB - more.shape[1])))

    d_q, d_k, d_v, d_bias = attention_backward(
        queries, keys, values, live, expo, inverse, context, d_context, 0, PAIRS
    )
    d_q, d_k, d_v, out_all = together(d_q, d_k, d_v, out_all)
    d_table = jnp.einsum("hrx,rxb->bh", d_bias, one_hot(grad_buckets()), precision=PRECISE)
    d_table = jnp.pad(
        d_table.reshape(experts, table_rows, HEADS), ((0, 0), (0, shard_rows - table_rows), (0, 0))
    ).reshape(D, HEADS)
    more = jnp.concatenate([d_router, d_gain_ffn[:, None], d_table], axis=1)
    more = jnp.pad(more, ((0, 0), (0, SUB - more.shape[1])))
    d_query, d_key, d_value = (
        dot_tn(n, d) for n, d in ((normed_one, d_q), (normed_span, d_k), (normed_span, d_v))
    )
    grads = [
        jnp.concatenate([in_rows(g.astype(jnp.bfloat16)) for g in pair], axis=1)
        for pair in ((d_query, d_attn_out, more), (d_key, d_value))
    ]
    mass = jnp.sum(router_probs * is_live, axis=0)
    mass_all, *grads = together(mass, *grads)
    for hop in range(bits_of("shard") + bits_of("seq")):
        axis, bit = scatter_order(0)[hop]
        mass_all = mass_all + exchange(mass_all, axis, 1 << bit)
        mass_all, *grads = together(mass_all, *scatter_hop(grads, hop))
        if hop == 0 and rep_count == 2:
            *grads, x_other[0] = together(*grads, x_other[0])
            rows_other = (x_other, hidden[2::3], hidden[0::3], hidden[1::3])
            d_expert = weight_pass(rows_other, d_expert, 1)
        if hop == 1:
            *grads, d_q, d_k, d_v = together(*grads, d_q, d_k, d_v)
        if hop == 2:
            *grads, out_all = together(*grads, out_all)
    d_span = dot_nt(d_k, w_k) + dot_nt(d_v, w_v)
    d_own = d_span[HALF : HALF + rows] + dot_nt(d_q, w_q)
    from_above = lax.ppermute(d_span[:HALF].astype(jnp.bfloat16), "seq", down)
    from_below = lax.ppermute(d_span[HALF + rows :].astype(jnp.bfloat16), "seq", up)
    if rep_count != 2:
        d_expert = [
            lax.psum(g.astype(jnp.bfloat16), "rep").astype(jnp.float32) for g in d_expert
        ]
    left, right = (rep_sums(g) for g in grads)
    for bit in range(bits_of("rep")):
        mass_all = mass_all + exchange(mass_all, "rep", 1 << bit)
    d_query, d_attn_out, more = left[:, :D], left[:, D : 2 * D], left[:, 2 * D :]
    d_key, d_value = right[:, :D], right[:, D:]
    d_gain_attn = sum(
        jnp.sum(g * w.astype(jnp.float32), axis=1)
        for g, w in ((d_query, w_query), (d_key, w_key), (d_value, w_value))
    ) / gain_attn.astype(jnp.float32)
    balance = experts * jnp.sum(shares * mass_all) / live_all
    importance = experts * mass_all / (rows * all_devices)
    expert_rows = collected(split(out_all))
    mixed = (hidden_state + gating[:, None] * expert_rows).astype(jnp.bfloat16)
    gap = jnp.zeros((rows - HALF, D), jnp.float32)
    d_normed_one = (
        d_own
        + jnp.concatenate([from_below.astype(jnp.float32), gap], axis=0)
        + jnp.concatenate([gap, from_above.astype(jnp.float32)], axis=0)
    )
    _, attn_pull = jax.vjp(lambda v: rms_norm(v, g_attn), inputs)
    d_tokens = d_hidden + attn_pull(d_normed_one)[0]
    return (
        mixed,
        balance,
        importance,
        d_tokens,
        d_gain_attn,
        more[:, experts],
        d_query,
        d_key,
        d_value,
        d_attn_out,
        more[:table_rows, experts + 1 : experts + 1 + HEADS],
        more[:, :experts],
        d_expert[0][None],
        d_expert[1][None],
    )


def solution(mesh):
    split = P(EVERY, None)
    shared = P(GROUP, None)
    gains = P(GROUP)
    stacked = P(GROUP, None, None)
    weights = (shared,) * 6 + (stacked,) * 2
    return jax.shard_map(
        shards,
        mesh=mesh,
        in_specs=(split, P(("rep", "shard"), None), split, split, gains, gains) + weights,
        out_specs=(split, P(), P(), split, gains, gains) + weights,
        check_vma=False,
    )
```
